256 devices in a mesh: gx: 8 (over y, core), gy: 8 (over z), gz: 4 (over x).
Axes of the slice: x: 4, y: 4, z: 8, core: 2. Of those that a mesh axis runs over, the one named last changes fastest.
Arguments:
- right_side: float32 [256, 256, 512], P('gx', 'gy', 'gz'), may hold values from -8 to 8
- coefficient: float32 [256, 256, 512], P('gx', 'gy', 'gz'), may hold values from 0.1 to 10
Outputs:
- fine_solution: float32 [256, 256, 512], P('gx', 'gy', 'gz')
- coarse_side: float32 [8, 8, 16], P('gx', 'gy', 'gz')
The draws below stay inside these ranges and needn't reach their ends.
All inputs are finite; a program needn't handle non-finite values.
Results may differ from the reference program's by a relative error of at most 0.0001.
Values sent between devices are 32-bit elements; how exact they have to be, the bound alone decides.
A program may use at most 128 MiB of HBM per device.

```python
import math
import jax
import jax.numpy as jnp
from jax import lax

LEVELS = 5
SWEEPS = 4
NX = 256
NY = 256
NZ = 512


def level_of(rng, dims, split, least, largest):
    loudness = 1.0
    for axis_at, parts in split:
        heights = jax.random.uniform(jax.random.fold_in(jax.random.fold_in(rng, 6), axis_at), (parts,), jnp.float32, least / len(split), largest / len(split))
        loudness = loudness * jnp.repeat(jnp.exp(heights), dims[axis_at] // parts).reshape((-1,) + (1,) * (len(dims) - 1 - axis_at))
    return loudness


def noise(own_key, shape, spread, bound, pieces=(), kind=jnp.bfloat16):
    drawn = spread * jax.random.normal(own_key, shape, jnp.float32)
    if pieces:
        drawn = drawn * level_of(own_key, shape, pieces, -0.22, 0.18)
    return jnp.clip(drawn, -bound, bound).astype(kind)


def setup_inputs(seed: int = 0) -> dict:
    arg_keys = jax.random.split(jax.random.key(seed), 3)
    return {
        "right_side": noise(arg_keys[0], (NX, NY, NZ), 1.0, 8.0, ((0, 8), (1, 8), (2, 4)), jnp.float32),
        "coefficient": jnp.clip(jnp.exp(math.log(10.0) - 4.6051702 * jax.random.uniform(arg_keys[1], (NX, NY, NZ), jnp.float32) ** level_of(arg_keys[1], (NX, NY, NZ), ((0, 8), (1, 8), (2, 4)), -0.2, 0.2)), 0.1, 10.0),
    }


OMEGA = 0.8


def side_views(pad):
    return [pad[2:, 1:-1, 1:-1], pad[:-2, 1:-1, 1:-1], pad[1:-1, 2:, 1:-1],
            pad[1:-1, :-2, 1:-1], pad[1:-1, 1:-1, 2:], pad[1:-1, 1:-1, :-2]]


def diagonal_of(kpad):
    centre = kpad[1:-1, 1:-1, 1:-1]
    others = side_views(kpad)
    faces = [0.5 * (centre + other) for other in others]
    return faces[0] + faces[1] + faces[2] + faces[3] + faces[4] + faces[5]


def neighbours(xpad, kpad):
    centre = kpad[1:-1, 1:-1, 1:-1]
    kother = side_views(kpad)
    xother = side_views(xpad)
    total = (0.5 * (centre + kother[0])) * xother[0]
    for index in range(1, 6):
        total = total + (0.5 * (centre + kother[index])) * xother[index]
    return total


def weigh_axis(extended, axis):
    length = extended.shape[axis]
    first = lax.slice_in_dim(extended, 0, length - 2, 2, axis)
    second = lax.slice_in_dim(extended, 1, length - 1, 2, axis)
    third = lax.slice_in_dim(extended, 2, length, 2, axis)
    fourth = lax.slice_in_dim(extended, 3, length, 2, axis)
    return (first + 3.0 * second + 3.0 * third + fourth) * 0.125


def restrict(rpad):
    return 4.0 * weigh_axis(weigh_axis(weigh_axis(rpad, 0), 1), 2)


def coarsen(coef):
    sx, sy, sz = coef.shape
    return jnp.mean(coef.reshape(sx // 2, 2, sy // 2, 2, sz // 2, 2), axis=(1, 3, 5))


def reference(right_side, coefficient):
    side, coef = right_side, coefficient
    fine_solution = None
    for level in range(LEVELS):
        kpad = jnp.pad(coef, 1)
        diag = diagonal_of(kpad)
        iterate = OMEGA * side / diag
        resid = side
        for sweep in range(SWEEPS):
            applied = diag * iterate - neighbours(jnp.pad(iterate, 1), kpad)
            resid = side - applied
            if sweep < SWEEPS - 1:
                iterate = iterate + OMEGA * resid / diag
        if level == 0:
            fine_solution = iterate
        side = restrict(jnp.pad(resid, 1))
        coef = coarsen(coef)
    return fine_solution, side
```

```python
import jax
import jax.numpy as jnp
from jax import lax
from jax.experimental import pallas as pl
from jax.experimental.pallas import tpu as pltpu
from jax.sharding import PartitionSpec as P

MESH = pl.DeviceIdType.MESH
F32 = jnp.float32
GX, GY, GZ = 8, 8, 4
HX = 6
RO = 16
LOCAL = ((32, 32, 128), (16, 16, 64), (8, 8, 32))
OFFSETS = [
    (dx, dy, dz) for dz in (0, 1, -1) for dy in (0, 1, -1) for dx in (0, 1, -1)
    if (dx, dy, dz) != (0, 0, 0)
]
OFFSETS.sort(key=lambda o: abs(o[0]) + abs(o[1]) + abs(o[2]))


def lane_ids(rows):
    return lax.broadcasted_iota(jnp.int32, (rows, 128), 1)


def loop(lo, hi, step, body):
    assert (hi - lo) % step == 0
    def run(j, carry):
        body(lo + j * step)
        return carry
    lax.fori_loop(0, (hi - lo) // step, run, 0)


def zshift(values):
    rows = values[0].shape[0]
    down = [pltpu.roll(v, 1, 1) for v in values]
    up = [pltpu.roll(v, 127, 1) for v in values]
    if len(values) == 1:
        return down, up
    lane = lane_ids(rows)
    first, last = lane == 0, lane == 127
    zm = [jnp.where(first, down[1], down[0]), jnp.where(first, down[0], down[1])]
    zp = [jnp.where(last, up[1], up[0]), jnp.where(last, up[0], up[1])]
    return zm, zp


def coef_pass(K, work, cs, kcs, lo, hi, r0, r1, chunk, unroll):
    A, Q, D = work["A"], work["Q"], work["D"]

    def body(i0):
        for i in [i0 + u for u in range(unroll)]:
            for r in range(r0, r1, chunk):
                rows = pl.ds(r, chunk)
                ks = [K[i, kc, rows, :] for kc in kcs]
                zm, zp = zshift(ks)
                for n, (c, kc) in enumerate(zip(cs, kcs)):
                    k = ks[n]
                    g = [
                        k + K[i + 1, kc, rows, :],
                        k + K[i - 1, kc, rows, :],
                        k + K[i, kc, pl.ds(r + 1, chunk), :],
                        k + K[i, kc, pl.ds(r - 1, chunk), :],
                        k + zp[n],
                        k + zm[n],
                    ]
                    total = (g[0] + g[1]) + (g[2] + g[3]) + (g[4] + g[5])
                    inside = k > 0.0
                    q = jnp.where(inside, 0.8 / total, 0.0)
                    for j in range(6):
                        A[j, i, c, rows, :] = q * g[j]
                    Q[i, c, rows, :] = 2.0 * q
                    D[i, c, rows, :] = jnp.where(inside, 0.625 * total, 0.0)

    loop(lo, hi, unroll, body)


def first_pass(B, work, cs, kcs, lo, hi, r0, r1, unroll):
    Q, C = work["Q"], work["C"]
    rows = pl.ds(r0, r1 - r0)

    def body(i0):
        for i in [i0 + u for u in range(unroll)]:
            for c, kc in zip(cs, kcs):
                C[i, c, rows, :] = Q[i, c, rows, :] * B[i, kc, rows, :]

    loop(lo, hi, unroll, body)


def sweep(X, OUT, work, cs, lo, hi, r0, r1, chunk, unroll, resid):
    A, C, D = work["A"], work["C"], work["D"]

    def body(i0):
        for i in [i0 + u for u in range(unroll)]:
            for r in range(r0, r1, chunk):
                rows = pl.ds(r, chunk)
                vs = [X[i, c, rows, :] for c in cs]
                zm, zp = zshift(vs)
                for n, c in enumerate(cs):
                    s = A[0, i, c, rows, :] * X[i + 1, c, rows, :]
                    s = s + A[1, i, c, rows, :] * X[i - 1, c, rows, :]
                    t = A[2, i, c, rows, :] * X[i, c, pl.ds(r + 1, chunk), :]
                    t = t + A[3, i, c, rows, :] * X[i, c, pl.ds(r - 1, chunk), :]
                    u = A[4, i, c, rows, :] * zp[n] + A[5, i, c, rows, :] * zm[n]
                    total = C[i, c, rows, :] + (s + t) + u
                    if resid:
                        OUT[i, c, rows, :] = D[i, c, rows, :] * (total - 0.8 * vs[n])
                    else:
                        OUT[i, c, rows, :] = total + 0.2 * vs[n]

    loop(lo, hi, unroll, body)


def weights(nz, tile, full):
    lane = lax.broadcasted_iota(jnp.int32, (128, 128), 0)
    coarse = lax.broadcasted_iota(jnp.int32, (128, 128), 1)
    if nz == 128:
        z = lane if tile == 0 else jnp.where(lane < 64, lane + 128, lane - 128)
    else:
        z = jnp.where(lane >= 120, lane - 128, lane)
    delta = z - 2 * coarse
    used = coarse < nz // 2
    inner = used & (delta >= 0) & (delta <= 1)
    if not full:
        return jnp.where(inner, 0.125, 0.0).astype(F32)
    outer = used & ((delta == -1) | (delta == 2))
    return jnp.where(inner, 3.0 / 128.0, jnp.where(outer, 1.0 / 128.0, 0.0)).astype(F32)


def matmul(a, b):
    return jnp.dot(a, b, precision=lax.Precision.HIGHEST, preferred_element_type=F32)


def restrict(R, work, cs, n, base):
    nx, ny, nz = n
    T, S = work["T"], work["S"]
    hy = ny // 2
    lo, size = 8, ny + 16

    def body(I):
        rows = pl.ds(lo, size)
        for c in cs:
            p = base + 2 * I
            T[I, c, rows, :] = (R[p, c, rows, :] + R[p + 3, c, rows, :]) + 3.0 * (
                R[p + 1, c, rows, :] + R[p + 2, c, rows, :])

    loop(0, nx // 2, 1, body)

    def weigh(I, at):
        for m, c in enumerate(cs):
            e = [T[I, c, pl.ds(RO - 1 + j, hy, stride=2), :] for j in range(4)]
            S[m, at, :] = (e[0] + e[3]) + 3.0 * (e[1] + e[2])

    if hy % 8 == 0:
        loop(0, nx // 2, 1, lambda I: weigh(I, pl.ds(pl.multiple_of(I * hy, 8), hy)))
    else:
        for I in range(nx // 2):
            weigh(I, pl.ds(I * hy, hy))
    count = (nx // 2) * hy
    total = matmul(S[0, :count, :], weights(nz, 0, True))
    if len(cs) == 2:
        total = total + matmul(S[1, :count, :], weights(nz, 1, True))
    return total


def coarsen(K, work, n, base):
    nx, ny, nz = n
    T, S = work["T"], work["S"]
    hy = ny // 2
    rows = pl.ds(RO, ny)

    def body(I):
        T[I, 0, rows, :] = K[base + 2 * I, 0, rows, :] + K[base + 2 * I + 1, 0, rows, :]

    loop(0, nx // 2, 1, body)

    def weigh(I, at):
        e = [T[I, 0, pl.ds(RO + j, hy, stride=2), :] for j in range(2)]
        S[0, at, :] = e[0] + e[1]

    if hy % 8 == 0:
        loop(0, nx // 2, 1, lambda I: weigh(I, pl.ds(pl.multiple_of(I * hy, 8), hy)))
    else:
        for I in range(nx // 2):
            weigh(I, pl.ds(I * hy, hy))
    return matmul(S[0, : (nx // 2) * hy, :], weights(nz, 0, False))


def place(dst, value, n, base):
    nx, ny = n[0], n[1]
    for x in range(nx):
        dst[base + x, 0, pl.ds(RO, ny), :] = value[x * ny:(x + 1) * ny, :]


def pack_z(A, pack, n):
    nx, ny, nz = n
    gs = min(16, nx)
    lane = lane_ids(ny)

    def body(g):
        hi = jnp.zeros((ny, 128), F32)
        lo = jnp.zeros((ny, 128), F32)
        for x in range(gs):
            v = A[HX + g * gs + x, 0, pl.ds(RO, ny), :]
            here = (lane >= 8 * x) & (lane < 8 * x + 8)
            hi = jnp.where(here, pltpu.roll(v, (8 * x - nz + 8) % 128, 1), hi)
            lo = jnp.where(here, pltpu.roll(v, 8 * x, 1) if x else v, lo)
        pack[0, g, :, :] = hi
        pack[1, g, :, :] = lo

    loop(0, nx // gs, 1, body)


def unpack_z(A, got, n, keep_lo, keep_hi):
    nx, ny, nz = n
    gs = min(16, nx)
    rows = ny + 16
    lane = lane_ids(rows)
    start = nz % 128
    from_lo = (lane >= 120) & keep_lo
    from_hi = (lane >= start) & (lane < start + 8) & keep_hi

    def body(i):
        xe = i - HX + gs
        g = xe // gs
        at = lax.rem(xe, gs) * 8
        lo = pltpu.roll(got[0, g, :, :], 120 - at, 1)
        hi = pltpu.roll(got[1, g, :, :], lax.rem(start - at + 128, 128), 1)
        if nz == 128:
            own = jnp.zeros((rows, 128), F32)
            A[i, 1, pl.ds(8, rows), :] = jnp.where(from_lo, lo, jnp.where(from_hi, hi, own))
        else:
            own = A[i, 0, pl.ds(8, rows), :]
            A[i, 0, pl.ds(8, rows), :] = jnp.where(from_lo, lo, jnp.where(from_hi, hi, own))

    loop(0, nx + 2 * HX, 1, body)


def halo_copies(A, pack, got, ssem, rsem, n, me):
    nx, ny, _ = n
    gs = min(16, nx)
    ng = nx // gs
    xs = {0: (pl.ds(HX, nx), pl.ds(HX, nx)), 1: (pl.ds(nx, HX), pl.ds(0, HX)),
          -1: (pl.ds(HX, HX), pl.ds(nx + HX, HX))}
    ys = {0: (pl.ds(RO, ny), pl.ds(RO, ny)), 1: (pl.ds(RO + ny - 8, 8), pl.ds(8, 8)),
          -1: (pl.ds(RO, 8), pl.ds(RO + ny, 8))}
    gxs = {0: (pl.ds(0, ng), pl.ds(1, ng)), 1: (pl.ds(ng - 1, 1), pl.ds(0, 1)),
           -1: (pl.ds(0, 1), pl.ds(ng + 1, 1))}
    pys = {0: (pl.ds(0, ny), pl.ds(8, ny)), 1: (pl.ds(ny - 8, 8), pl.ds(0, 8)),
           -1: (pl.ds(0, 8), pl.ds(8 + ny, 8))}
    copies = []
    for j, (dx, dy, dz) in enumerate(OFFSETS):
        if dz == 0:
            src = A.at[xs[dx][0], 0, ys[dy][0], :]
            dst = A.at[xs[dx][1], 0, ys[dy][1], :]
        else:
            side = 0 if dz == 1 else 1
            src = pack.at[side, gxs[dx][0], pys[dy][0], :]
            dst = got.at[side, gxs[dx][1], pys[dy][1], :]
        copies.append(pltpu.make_async_remote_copy(
            src_ref=src, dst_ref=dst, send_sem=ssem.at[j], recv_sem=rsem.at[j],
            device_id=peer(me, (dx, dy, dz)), device_id_type=MESH))
    return copies


def peer(me, offset):
    return tuple(lax.rem(m + o + s, s) for m, o, s in zip(me, offset, (GX, GY, GZ)))


def start(copies):
    for copy in copies:
        copy.start()


def clear_outside(K, n, me):
    nx, ny, nz = n
    tiles = 2 if nz == 128 else 1

    def planes(first):
        K[pl.ds(first, HX), :, :, :] = jnp.zeros((HX, tiles, ny + 32, 128), F32)

    def rows(first):
        K[:, :, pl.ds(first, 8), :] = jnp.zeros((nx + 2 * HX, tiles, 8, 128), F32)

    pl.when(me[0] == 0)(lambda: planes(0))
    pl.when(me[0] == GX - 1)(lambda: planes(nx + HX))
    pl.when(me[1] == 0)(lambda: rows(8))
    pl.when(me[1] == GY - 1)(lambda: rows(RO + ny))


def kernel(b_hbm, k_hbm, fine_hbm, out_ref, K0, B0, K1, B1, K2, B2, K3, B3, K4, B4,
           A, Q, D, C, XA, XB, T, S, PS0, PR0, PS1, PR1, PS2, PR2, ZS, ZR, G, FIN,
           lsem, ssem, rsem, gssem, grsem):
    me = (lax.axis_index("gx"), lax.axis_index("gy"), lax.axis_index("gz"))
    gx, gy, gz = me
    work = {"A": A, "Q": Q, "D": D, "C": C, "T": T, "S": S}
    n0, n1, n2 = LOCAL
    keep_lo, keep_hi = gz > 0, gz < GZ - 1

    own = (pl.ds(HX, 32), 0, pl.ds(RO, 32), slice(None))
    load_k = pltpu.make_async_copy(k_hbm, K0.at[own], lsem.at[0])
    load_b = pltpu.make_async_copy(b_hbm, B0.at[own], lsem.at[1])
    load_k.start()
    load_b.start()

    partners = list(OFFSETS)
    partners += [(d, 0, 0) for d in range(2, GX - 1)]
    partners += [(0, d, 0) for d in range(2, GY - 1)]
    partners += [(0, 0, 2)]
    barrier = pltpu.get_barrier_semaphore()
    for offset in partners:
        pl.semaphore_signal(barrier, inc=1, device_id=peer(me, offset), device_id_type=MESH)

    load_k.wait()
    pack_z(K0, PS0.at[0], n0)
    pl.semaphore_wait(barrier, len(partners))
    k0 = halo_copies(K0, PS0.at[0], PR0.at[0], ssem.at[0], rsem.at[0], n0, me)
    start(k0)
    load_b.wait()
    pack_z(B0, PS0.at[1], n0)
    b0 = halo_copies(B0, PS0.at[1], PR0.at[1], ssem.at[1], rsem.at[1], n0, me)
    start(b0)

    def gather_copies(s):
        z = [pltpu.make_async_remote_copy(
            src_ref=ZS.at[s], dst_ref=ZR.at[s, o - 1], send_sem=gssem.at[s, o - 1],
            recv_sem=grsem.at[s, o - 1], device_id=peer(me, (0, 0, o)), device_id_type=MESH)
            for o in range(1, GZ)]
        y = [pltpu.make_async_remote_copy(
            src_ref=G.at[s, gx, gy], dst_ref=G.at[s, gx, gy], send_sem=gssem.at[s, 2 + o],
            recv_sem=grsem.at[s, 2 + o], device_id=peer(me, (0, o, 0)), device_id_type=MESH)
            for o in range(1, GY)]
        x = [pltpu.make_async_remote_copy(
            src_ref=G.at[s, gx], dst_ref=G.at[s, gx], send_sem=gssem.at[s, 9 + o],
            recv_sem=grsem.at[s, 9 + o], device_id=peer(me, (o, 0, 0)), device_id_type=MESH)
            for o in range(1, GX)]
        return z, y, x

    gk, gb = gather_copies(0), gather_copies(1)

    def gather_z(s, copies, rows):
        placed = pltpu.roll(rows, 16 * gz, 1)
        ZS[s, :, :] = placed[:8, :] + pltpu.roll(placed[8:, :], 64, 1)
        start(copies[0])

    def gather_y(s, copies):
        for copy in copies[0]:
            copy.wait_recv()
        G[s, gx, gy, :, :] = (ZS[s, :, :] + ZR[s, 0, :, :]) + (ZR[s, 1, :, :] + ZR[s, 2, :, :])
        start(copies[1])

    def gather_x(copies):
        for copy in copies[1]:
            copy.wait_recv()
        start(copies[2])

    def gather_end(s, copies, dst):
        for copy in copies[2]:
            copy.wait_recv()
        lower = lane_ids(4) < 64

        def body(g):
            for y in range(GY):
                for x in range(4):
                    v = G[s, g, y, pl.ds((x % 2) * 4, 4), :]
                    if x >= 2:
                        v = pltpu.roll(v, 64, 1)
                    dst[1 + 4 * g + x, 0, pl.ds(RO + 4 * y, 4), :] = jnp.where(lower, v, 0.0)

        loop(0, GX, 1, body)
        for group in copies:
            for copy in group:
                copy.wait_send()

    place(K1, coarsen(K0, work, n0, HX), n1, HX)
    pack_z(K1, PS1.at[0], n1)
    k1 = halo_copies(K1, PS1.at[0], PR1.at[0], ssem.at[2], rsem.at[2], n1, me)
    start(k1)
    place(K2, coarsen(K1, work, n1, HX), n2, HX)
    pack_z(K2, PS2.at[0], n2)
    k2 = halo_copies(K2, PS2.at[0], PR2.at[0], ssem.at[4], rsem.at[4], n2, me)
    start(k2)
    gather_z(0, gk, coarsen(K2, work, n2, HX))
    K3[...] = jnp.zeros(K3.shape, F32)
    K4[...] = jnp.zeros(K4.shape, F32)

    def land(copies, dst, got, n, is_k):
        for copy in copies:
            copy.wait_recv()
        for copy in copies:
            copy.wait_send()
        unpack_z(dst, got, n, keep_lo, keep_hi)
        if is_k:
            clear_outside(dst, n, me)

    def wide(n, K, B, cs, kcs, kc, bc, got, chunk, unroll):
        nx, ny, _ = n
        r0, r1 = 8, ny + 24
        land(kc, K, got.at[0], n, True)
        coef_pass(K, work, cs, kcs, 1, nx + 11, r0, r1, chunk, 1)
        land(bc, B, got.at[1], n, False)
        first_pass(B, work, cs, kcs, 1, nx + 11, r0, r1, 1)
        sweep(C, XA, work, cs, 2, nx + 10, r0, r1, chunk, unroll, False)
        sweep(XA, XB, work, cs, 3, nx + 9, r0, r1, chunk, unroll, False)
        sweep(XB, XA, work, cs, 4, nx + 8, r0, r1, chunk, unroll, False)

    def resid_wide(n, cs, chunk, unroll):
        nx, ny, _ = n
        sweep(XA, XB, work, cs, 5, nx + 7, 8, ny + 24, chunk, unroll, True)
        return restrict(XB, work, cs, n, HX - 1)

    wide(n0, K0, B0, (0, 1), (0, 1), k0, b0, PR0, 16, 1)
    store = pltpu.make_async_copy(XA.at[own], fine_hbm, lsem.at[2])
    store.start()
    gather_y(0, gk)
    place(B1, resid_wide(n0, (0, 1), 16, 1), n1, HX)
    pack_z(B1, PS1.at[1], n1)
    b1 = halo_copies(B1, PS1.at[1], PR1.at[1], ssem.at[3], rsem.at[3], n1, me)
    start(b1)
    store.wait()
    wide(n1, K1, B1, (0,), (0,), k1, b1, PR1, 32, 2)
    gather_x(gk)
    place(B2, resid_wide(n1, (0,), 32, 2), n2, HX)
    pack_z(B2, PS2.at[1], n2)
    b2 = halo_copies(B2, PS2.at[1], PR2.at[1], ssem.at[5], rsem.at[5], n2, me)
    start(b2)
    wide(n2, K2, B2, (0,), (0,), k2, b2, PR2, 24, 2)
    gather_z(1, gb, resid_wide(n2, (0,), 24, 2))

    n3, n4 = (32, 32, 64), (16, 16, 32)
    gather_end(0, gk, K3)
    gather_y(1, gb)

    def whole_prepare(n, K, c):
        nx, ny, _ = n
        for X in (C, XA, XB):
            for p in (0, nx + 1):
                X[p, c, pl.ds(8, ny + 16), :] = jnp.zeros((ny + 16, 128), F32)
            for r in (8, RO + ny):
                X[pl.ds(1, nx), c, pl.ds(r, 8), :] = jnp.zeros((nx, 8, 128), F32)
        coef_pass(K, work, (c,), (0,), 1, nx + 1, RO, RO + ny, ny, 1)

    def whole(n, B, c):
        nx, ny, _ = n
        span = (1, nx + 1, RO, RO + ny)
        first_pass(B, work, (c,), (0,), *span, 2)
        sweep(C, XA, work, (c,), *span, ny, 2, False)
        sweep(XA, XB, work, (c,), *span, ny, 2, False)
        sweep(XB, XA, work, (c,), *span, ny, 2, False)
        sweep(XA, XB, work, (c,), *span, ny, 2, True)
        return restrict(XB, work, (c,), n, 0)

    whole_prepare(n3, K3, 0)
    gather_x(gb)
    place(K4, coarsen(K3, work, n3, 1), n4, 1)
    whole_prepare(n4, K4, 1)
    gather_end(1, gb, B3)
    place(B4, whole(n3, B3, 0), n4, 1)
    FIN[...] = whole(n4, B4, 1)
    row = FIN[pl.ds(gx * 8 + gy, 1), :]
    out_ref[0, :, :] = pltpu.roll(row, lax.rem(128 - 4 * gz, 128), 1)[:, :4]


def local(right_side, coefficient):
    def vm(*shape):
        return pltpu.VMEM(shape, F32)

    dma = pltpu.SemaphoreType.DMA
    scratch = [
        vm(44, 2, 64, 128), vm(44, 2, 64, 128),
        vm(28, 1, 48, 128), vm(28, 1, 48, 128),
        vm(20, 1, 40, 128), vm(20, 1, 40, 128),
        vm(34, 1, 64, 128), vm(34, 1, 64, 128),
        vm(18, 1, 48, 128), vm(18, 1, 48, 128),
        vm(6, 44, 2, 64, 128),
    ] + [vm(44, 2, 64, 128) for _ in range(5)] + [
        vm(16, 2, 64, 128), vm(2, 256, 128),
        vm(2, 2, 2, 32, 128), vm(2, 2, 4, 48, 128),
        vm(2, 2, 1, 16, 128), vm(2, 2, 3, 32, 128),
        vm(2, 2, 1, 8, 128), vm(2, 2, 3, 24, 128),
        vm(2, 8, 128), vm(2, 3, 8, 128), vm(2, GX, GY, 8, 128), vm(64, 128),
        dma((3,)), dma((6, 26)), dma((6, 26)), dma((2, 17)), dma((2, 17)),
    ]
    hbm = pl.BlockSpec(memory_space=pl.ANY)
    return pl.pallas_call(
        kernel,
        out_shape=(
            jax.ShapeDtypeStruct(right_side.shape, F32),
            jax.ShapeDtypeStruct((1, 1, 4), F32),
        ),
        in_specs=[hbm, hbm],
        out_specs=(hbm, pl.BlockSpec(memory_space=pltpu.VMEM)),
        scratch_shapes=scratch,
        compiler_params=pltpu.CompilerParams(
            collective_id=0, has_side_effects=True, vmem_limit_bytes=56 * 2**20),
        name="down_leg",
    )(right_side, coefficient)


def solution(mesh):
    placed = (P("gx", "gy", "gz"), P("gx", "gy", "gz"))
    return jax.shard_map(
        local, mesh=mesh, in_specs=placed, out_specs=placed, check_vma=False)
```

```python
import jax
import jax.numpy as jnp
from jax import lax
from jax.experimental import pallas as pl
from jax.experimental.pallas import tpu as pltpu
from jax.sharding import PartitionSpec as P

MESH = pl.DeviceIdType.MESH
F32 = jnp.float32
GX, GY, GZ = 8, 8, 4
HX = 6
RO = 16
LOCAL = ((32, 32, 128), (16, 16, 64), (8, 8, 32))
OFFSETS = [
    (dx, dy, dz) for dz in (0, 1, -1) for dy in (0, 1, -1) for dx in (0, 1, -1)
    if (dx, dy, dz) != (0, 0, 0)
]
OFFSETS.sort(key=lambda o: abs(o[0]) + abs(o[1]) + abs(o[2]))


def lane_ids(rows):
    return lax.broadcasted_iota(jnp.int32, (rows, 128), 1)


def loop(lo, hi, step, body):
    assert (hi - lo) % step == 0
    def run(j, carry):
        body(lo + j * step)
        return carry
    lax.fori_loop(0, (hi - lo) // step, run, 0)


def zshift(values):
    rows = values[0].shape[0]
    down = [pltpu.roll(v, 1, 1) for v in values]
    up = [pltpu.roll(v, 127, 1) for v in values]
    if len(values) == 1:
        return down, up
    lane = lane_ids(rows)
    first, last = lane == 0, lane == 127
    zm = [jnp.where(first, down[1], down[0]), jnp.where(first, down[0], down[1])]
    zp = [jnp.where(last, up[1], up[0]), jnp.where(last, up[0], up[1])]
    return zm, zp


def coef_pass(K, work, cs, kcs, lo, hi, r0, r1, chunk, unroll):
    A, Q, D = work["A"], work["Q"], work["D"]

    def body(i0):
        for i in [i0 + u for u in range(unroll)]:
            for r in range(r0, r1, chunk):
                rows = pl.ds(r, chunk)
                ks = [K[i, kc, rows, :] for kc in kcs]
                zm, zp = zshift(ks)
                for n, (c, kc) in enumerate(zip(cs, kcs)):
                    k = ks[n]
                    g = [
                        k + K[i + 1, kc, rows, :],
                        k + K[i - 1, kc, rows, :],
                        k + K[i, kc, pl.ds(r + 1, chunk), :],
                        k + K[i, kc, pl.ds(r - 1, chunk), :],
                        k + zp[n],
                        k + zm[n],
                    ]
                    total = (g[0] + g[1]) + (g[2] + g[3]) + (g[4] + g[5])
                    inside = k > 0.0
                    q = jnp.where(inside, 0.8 / total, 0.0)
                    for j in range(6):
                        A[j, i, c, rows, :] = q * g[j]
                    Q[i, c, rows, :] = 2.0 * q
                    D[i, c, rows, :] = jnp.where(inside, 0.625 * total, 0.0)

    loop(lo, hi, unroll, body)


def first_pass(B, work, cs, kcs, lo, hi, r0, r1, unroll):
    Q, C = work["Q"], work["C"]
    rows = pl.ds(r0, r1 - r0)

    def body(i0):
        for i in [i0 + u for u in range(unroll)]:
            for c, kc in zip(cs, kcs):
                C[i, c, rows, :] = Q[i, c, rows, :] * B[i, kc, rows, :]

    loop(lo, hi, unroll, body)


def sweep(X, OUT, work, cs, lo, hi, r0, r1, chunk, unroll, resid):
    A, C, D = work["A"], work["C"], work["D"]

    def body(i0):
        for i in [i0 + u for u in range(unroll)]:
            for r in range(r0, r1, chunk):
                rows = pl.ds(r, chunk)
                vs = [X[i, c, rows, :] for c in cs]
                zm, zp = zshift(vs)
                for n, c in enumerate(cs):
                    s = A[0, i, c, rows, :] * X[i + 1, c, rows, :]
                    s = s + A[1, i, c, rows, :] * X[i - 1, c, rows, :]
                    t = A[2, i, c, rows, :] * X[i, c, pl.ds(r + 1, chunk), :]
                    t = t + A[3, i, c, rows, :] * X[i, c, pl.ds(r - 1, chunk), :]
                    u = A[4, i, c, rows, :] * zp[n] + A[5, i, c, rows, :] * zm[n]
                    total = C[i, c, rows, :] + (s + t) + u
                    if resid:
                        OUT[i, c, rows, :] = D[i, c, rows, :] * (total - 0.8 * vs[n])
                    else:
                        OUT[i, c, rows, :] = total + 0.2 * vs[n]

    loop(lo, hi, unroll, body)


def weights(nz, tile, full):
    lane = lax.broadcasted_iota(jnp.int32, (128, 128), 0)
    coarse = lax.broadcasted_iota(jnp.int32, (128, 128), 1)
    if nz == 128:
        z = lane if tile == 0 else jnp.where(lane < 64, lane + 128, lane - 128)
    else:
        z = jnp.where(lane >= 120, lane - 128, lane)
    delta = z - 2 * coarse
    used = coarse < nz // 2
    inner = used & (delta >= 0) & (delta <= 1)
    if not full:
        return jnp.where(inner, 0.125, 0.0).astype(F32)
    outer = used & ((delta == -1) | (delta == 2))
    return jnp.where(inner, 3.0 / 128.0, jnp.where(outer, 1.0 / 128.0, 0.0)).astype(F32)


def matmul(a, b):
    return jnp.dot(a, b, precision=lax.Precision.HIGHEST, preferred_element_type=F32)


def restrict(R, work, cs, n, base):
    nx, ny, nz = n
    T, S = work["T"], work["S"]
    hy = ny // 2
    lo, size = 8, ny + 16

    def body(I):
        rows = pl.ds(lo, size)
        for c in cs:
            p = base + 2 * I
            T[I, c, rows, :] = (R[p, c, rows, :] + R[p + 3, c, rows, :]) + 3.0 * (
                R[p + 1, c, rows, :] + R[p + 2, c, rows, :])

    loop(0, nx // 2, 1, body)

    def weigh(I, at):
        for m, c in enumerate(cs):
            e = [T[I, c, pl.ds(RO - 1 + j, hy, stride=2), :] for j in range(4)]
            S[m, at, :] = (e[0] + e[3]) + 3.0 * (e[1] + e[2])

    if hy % 8 == 0:
        loop(0, nx // 2, 1, lambda I: weigh(I, pl.ds(pl.multiple_of(I * hy, 8), hy)))
    else:
        for I in range(nx // 2):
            weigh(I, pl.ds(I * hy, hy))
    count = (nx // 2) * hy
    total = matmul(S[0, :count, :], weights(nz, 0, True))
    if len(cs) == 2:
        total = total + matmul(S[1, :count, :], weights(nz, 1, True))
    return total


def coarsen(K, work, n, base):
    nx, ny, nz = n
    T, S = work["T"], work["S"]
    hy = ny // 2
    rows = pl.ds(RO, ny)

    def body(I):
        T[I, 0, rows, :] = K[base + 2 * I, 0, rows, :] + K[base + 2 * I + 1, 0, rows, :]

    loop(0, nx // 2, 1, body)

    def weigh(I, at):
        e = [T[I, 0, pl.ds(RO + j, hy, stride=2), :] for j in range(2)]
        S[0, at, :] = e[0] + e[1]

    if hy % 8 == 0:
        loop(0, nx // 2, 1, lambda I: weigh(I, pl.ds(pl.multiple_of(I * hy, 8), hy)))
    else:
        for I in range(nx // 2):
            weigh(I, pl.ds(I * hy, hy))
    return matmul(S[0, : (nx // 2) * hy, :], weights(nz, 0, False))


def place(dst, value, n, base):
    nx, ny = n[0], n[1]
    for x in range(nx):
        dst[base + x, 0, pl.ds(RO, ny), :] = value[x * ny:(x + 1) * ny, :]


def pack_z(A, pack, n):
    nx, ny, nz = n
    gs = min(16, nx)
    lane = lane_ids(ny)

    def body(g):
        hi = jnp.zeros((ny, 128), F32)
        lo = jnp.zeros((ny, 128), F32)
        for x in range(gs):
            v = A[HX + g * gs + x, 0, pl.ds(RO, ny), :]
            here = (lane >= 8 * x) & (lane < 8 * x + 8)
            hi = jnp.where(here, pltpu.roll(v, (8 * x - nz + 8) % 128, 1), hi)
            lo = jnp.where(here, pltpu.roll(v, 8 * x, 1) if x else v, lo)
        pack[0, g, :, :] = hi
        pack[1, g, :, :] = lo

    loop(0, nx // gs, 1, body)


def unpack_z(A, got, n, keep_lo, keep_hi):
    nx, ny, nz = n
    gs = min(16, nx)
    rows = ny + 16
    lane = lane_ids(rows)
    start = nz % 128
    from_lo = (lane >= 120) & keep_lo
    from_hi = (lane >= start) & (lane < start + 8) & keep_hi

    def body(i):
        xe = i - HX + gs
        g = xe // gs
        at = lax.rem(xe, gs) * 8
        lo = pltpu.roll(got[0, g, :, :], 120 - at, 1)
        hi = pltpu.roll(got[1, g, :, :], lax.rem(start - at + 128, 128), 1)
        if nz == 128:
            own = jnp.zeros((rows, 128), F32)
            A[i, 1, pl.ds(8, rows), :] = jnp.where(from_lo, lo, jnp.where(from_hi, hi, own))
        else:
            own = A[i, 0, pl.ds(8, rows), :]
            A[i, 0, pl.ds(8, rows), :] = jnp.where(from_lo, lo, jnp.where(from_hi, hi, own))

    loop(0, nx + 2 * HX, 4, lambda i0: [body(i0 + u) for u in range(4)])


def halo_copies(A, pack, got, ssem, rsem, n, me):
    nx, ny, _ = n
    gs = min(16, nx)
    ng = nx // gs
    xs = {0: (pl.ds(HX, nx), pl.ds(HX, nx)), 1: (pl.ds(nx, HX), pl.ds(0, HX)),
          -1: (pl.ds(HX, HX), pl.ds(nx + HX, HX))}
    ys = {0: (pl.ds(RO, ny), pl.ds(RO, ny)), 1: (pl.ds(RO + ny - 8, 8), pl.ds(8, 8)),
          -1: (pl.ds(RO, 8), pl.ds(RO + ny, 8))}
    gxs = {0: (pl.ds(0, ng), pl.ds(1, ng)), 1: (pl.ds(ng - 1, 1), pl.ds(0, 1)),
           -1: (pl.ds(0, 1), pl.ds(ng + 1, 1))}
    pys = {0: (pl.ds(0, ny), pl.ds(8, ny)), 1: (pl.ds(ny - 8, 8), pl.ds(0, 8)),
           -1: (pl.ds(0, 8), pl.ds(8 + ny, 8))}
    copies = []
    for j, (dx, dy, dz) in enumerate(OFFSETS):
        if dz == 0:
            src = A.at[xs[dx][0], 0, ys[dy][0], :]
            dst = A.at[xs[dx][1], 0, ys[dy][1], :]
        else:
            side = 0 if dz == 1 else 1
            src = pack.at[side, gxs[dx][0], pys[dy][0], :]
            dst = got.at[side, gxs[dx][1], pys[dy][1], :]
        copies.append(pltpu.make_async_remote_copy(
            src_ref=src, dst_ref=dst, send_sem=ssem.at[j], recv_sem=rsem.at[j],
            device_id=peer(me, (dx, dy, dz)), device_id_type=MESH))
    return copies


def peer(me, offset):
    return tuple(lax.rem(m + o + s, s) for m, o, s in zip(me, offset, (GX, GY, GZ)))


def start(copies):
    for copy in copies:
        copy.start()


def clear_outside(K, n, me):
    nx, ny, nz = n
    tiles = 2 if nz == 128 else 1

    def planes(first):
        K[pl.ds(first, HX), :, :, :] = jnp.zeros((HX, tiles, ny + 32, 128), F32)

    def rows(first):
        K[:, :, pl.ds(first, 8), :] = jnp.zeros((nx + 2 * HX, tiles, 8, 128), F32)

    pl.when(me[0] == 0)(lambda: planes(0))
    pl.when(me[0] == GX - 1)(lambda: planes(nx + HX))
    pl.when(me[1] == 0)(lambda: rows(8))
    pl.when(me[1] == GY - 1)(lambda: rows(RO + ny))


def kernel(b_hbm, k_hbm, fine_hbm, out_ref, K0, B0, K1, B1, K2, B2, K3, B3, K4, B4,
           A, Q, D, C, XA, XB, T, S, PS0, PR0, PS1, PR1, PS2, PR2, ZS, ZR, G, FIN,
           lsem, ssem, rsem, gssem, grsem):
    me = (lax.axis_index("gx"), lax.axis_index("gy"), lax.axis_index("gz"))
    gx, gy, gz = me
    work = {"A": A, "Q": Q, "D": D, "C": C, "T": T, "S": S}
    n0, n1, n2 = LOCAL
    keep_lo, keep_hi = gz > 0, gz < GZ - 1

    own = (pl.ds(HX, 32), 0, pl.ds(RO, 32), slice(None))
    load_k = pltpu.make_async_copy(k_hbm, K0.at[own], lsem.at[0])
    load_b = pltpu.make_async_copy(b_hbm, B0.at[own], lsem.at[1])
    load_k.start()
    load_b.start()

    partners = list(OFFSETS)
    partners += [(d, 0, 0) for d in range(2, GX - 1)]
    partners += [(0, d, 0) for d in range(2, GY - 1)]
    partners += [(0, 0, 2)]
    barrier = pltpu.get_barrier_semaphore()
    for offset in partners:
        pl.semaphore_signal(barrier, inc=1, device_id=peer(me, offset), device_id_type=MESH)

    load_k.wait()
    pack_z(K0, PS0.at[0], n0)
    pl.semaphore_wait(barrier, len(partners))
    k0 = halo_copies(K0, PS0.at[0], PR0.at[0], ssem.at[0], rsem.at[0], n0, me)
    start(k0)
    load_b.wait()
    pack_z(B0, PS0.at[1], n0)
    b0 = halo_copies(B0, PS0.at[1], PR0.at[1], ssem.at[1], rsem.at[1], n0, me)
    start(b0)

    def gather_copies(s):
        z = [pltpu.make_async_remote_copy(
            src_ref=ZS.at[s], dst_ref=ZR.at[s, o - 1], send_sem=gssem.at[s, o - 1],
            recv_sem=grsem.at[s, o - 1], device_id=peer(me, (0, 0, o)), device_id_type=MESH)
            for o in range(1, GZ)]
        y = [pltpu.make_async_remote_copy(
            src_ref=G.at[s, gx, gy], dst_ref=G.at[s, gx, gy], send_sem=gssem.at[s, 2 + o],
            recv_sem=grsem.at[s, 2 + o], device_id=peer(me, (0, o, 0)), device_id_type=MESH)
            for o in range(1, GY)]
        x = [pltpu.make_async_remote_copy(
            src_ref=G.at[s, gx], dst_ref=G.at[s, gx], send_sem=gssem.at[s, 9 + o],
            recv_sem=grsem.at[s, 9 + o], device_id=peer(me, (o, 0, 0)), device_id_type=MESH)
            for o in range(1, GX)]
        return z, y, x

    gk, gb = gather_copies(0), gather_copies(1)

    def gather_z(s, copies, rows):
        placed = pltpu.roll(rows, 16 * gz, 1)
        ZS[s, :, :] = placed[:8, :] + pltpu.roll(placed[8:, :], 64, 1)
        start(copies[0])

    def gather_y(s, copies):
        for copy in copies[0]:
            copy.wait_recv()
        G[s, gx, gy, :, :] = (ZS[s, :, :] + ZR[s, 0, :, :]) + (ZR[s, 1, :, :] + ZR[s, 2, :, :])
        start(copies[1])

    def gather_x(copies):
        for copy in copies[1]:
            copy.wait_recv()
        start(copies[2])

    def gather_end(s, copies, dst):
        for copy in copies[2]:
            copy.wait_recv()
        lower = lane_ids(4) < 64

        def body(g):
            for y in range(GY):
                for x in range(4):
                    v = G[s, g, y, pl.ds((x % 2) * 4, 4), :]
                    if x >= 2:
                        v = pltpu.roll(v, 64, 1)
                    dst[1 + 4 * g + x, 0, pl.ds(RO + 4 * y, 4), :] = jnp.where(lower, v, 0.0)

        loop(0, GX, 1, body)
        for group in copies:
            for copy in group:
                copy.wait_send()

    place(K1, coarsen(K0, work, n0, HX), n1, HX)
    pack_z(K1, PS1.at[0], n1)
    k1 = halo_copies(K1, PS1.at[0], PR1.at[0], ssem.at[2], rsem.at[2], n1, me)
    start(k1)
    place(K2, coarsen(K1, work, n1, HX), n2, HX)
    pack_z(K2, PS2.at[0], n2)
    k2 = halo_copies(K2, PS2.at[0], PR2.at[0], ssem.at[4], rsem.at[4], n2, me)
    start(k2)
    gather_z(0, gk, coarsen(K2, work, n2, HX))
    K3[...] = jnp.zeros(K3.shape, F32)
    K4[...] = jnp.zeros(K4.shape, F32)

    def land(copies, dst, got, n, is_k):
        for copy in copies:
            copy.wait_recv()
        for copy in copies:
            copy.wait_send()
        unpack_z(dst, got, n, keep_lo, keep_hi)
        if is_k:
            clear_outside(dst, n, me)

    def wide(n, K, B, cs, kcs, kc, bc, got, chunk, steps):
        nx, ny, _ = n
        r0, r1 = 8, ny + 24
        land(kc, K, got.at[0], n, True)
        coef_pass(K, work, cs, kcs, 1, nx + 11, r0, r1, chunk, steps[0])
        land(bc, B, got.at[1], n, False)
        first_pass(B, work, cs, kcs, 1, nx + 11, r0, r1, steps[0])
        sweep(C, XA, work, cs, 2, nx + 10, r0, r1, chunk, steps[1], False)
        sweep(XA, XB, work, cs, 2, nx + 10, r0, r1, chunk, steps[1], False)
        sweep(XB, XA, work, cs, 4, nx + 8, r0, r1, chunk, steps[2], False)

    def resid_wide(n, cs, chunk, step):
        nx, ny, _ = n
        sweep(XA, XB, work, cs, 4, nx + 8, 8, ny + 24, chunk, step, True)
        return restrict(XB, work, cs, n, HX - 1)

    wide(n0, K0, B0, (0, 1), (0, 1), k0, b0, PR0, 16, (6, 8, 9))
    store = pltpu.make_async_copy(XA.at[own], fine_hbm, lsem.at[2])
    store.start()
    gather_y(0, gk)
    place(B1, resid_wide(n0, (0, 1), 16, 9), n1, HX)
    pack_z(B1, PS1.at[1], n1)
    b1 = halo_copies(B1, PS1.at[1], PR1.at[1], ssem.at[3], rsem.at[3], n1, me)
    start(b1)
    store.wait()
    wide(n1, K1, B1, (0,), (0,), k1, b1, PR1, 32, (13, 8, 10))
    gather_x(gk)
    place(B2, resid_wide(n1, (0,), 32, 10), n2, HX)
    pack_z(B2, PS2.at[1], n2)
    b2 = halo_copies(B2, PS2.at[1], PR2.at[1], ssem.at[5], rsem.at[5], n2, me)
    start(b2)
    wide(n2, K2, B2, (0,), (0,), k2, b2, PR2, 24, (9, 8, 6))
    gather_z(1, gb, resid_wide(n2, (0,), 24, 6))

    n3, n4 = (32, 32, 64), (16, 16, 32)
    gather_end(0, gk, K3)
    gather_y(1, gb)

    def whole_prepare(n, K, c):
        nx, ny, _ = n
        for X in (C, XA, XB):
            for p in (0, nx + 1):
                X[p, c, pl.ds(8, ny + 16), :] = jnp.zeros((ny + 16, 128), F32)
            for r in (8, RO + ny):
                X[pl.ds(1, nx), c, pl.ds(r, 8), :] = jnp.zeros((nx, 8, 128), F32)
        coef_pass(K, work, (c,), (0,), 1, nx + 1, RO, RO + ny, ny, 8)

    def whole(n, B, c):
        nx, ny, _ = n
        span = (1, nx + 1, RO, RO + ny)
        first_pass(B, work, (c,), (0,), *span, 8)
        sweep(C, XA, work, (c,), *span, ny, 8, False)
        sweep(XA, XB, work, (c,), *span, ny, 8, False)
        sweep(XB, XA, work, (c,), *span, ny, 8, False)
        sweep(XA, XB, work, (c,), *span, ny, 8, True)
        return restrict(XB, work, (c,), n, 0)

    whole_prepare(n3, K3, 0)
    gather_x(gb)
    place(K4, coarsen(K3, work, n3, 1), n4, 1)
    whole_prepare(n4, K4, 1)
    gather_end(1, gb, B3)
    place(B4, whole(n3, B3, 0), n4, 1)
    FIN[...] = whole(n4, B4, 1)
    row = FIN[pl.ds(gx * 8 + gy, 1), :]
    out_ref[0, :, :] = pltpu.roll(row, lax.rem(128 - 4 * gz, 128), 1)[:, :4]


def local(right_side, coefficient):
    def vm(*shape):
        return pltpu.VMEM(shape, F32)

    dma = pltpu.SemaphoreType.DMA
    scratch = [
        vm(44, 2, 64, 128), vm(44, 2, 64, 128),
        vm(28, 1, 48, 128), vm(28, 1, 48, 128),
        vm(20, 1, 40, 128), vm(20, 1, 40, 128),
        vm(34, 1, 64, 128), vm(34, 1, 64, 128),
        vm(18, 1, 48, 128), vm(18, 1, 48, 128),
        vm(6, 44, 2, 64, 128),
    ] + [vm(44, 2, 64, 128) for _ in range(5)] + [
        vm(16, 2, 64, 128), vm(2, 256, 128),
        vm(2, 2, 2, 32, 128), vm(2, 2, 4, 48, 128),
        vm(2, 2, 1, 16, 128), vm(2, 2, 3, 32, 128),
        vm(2, 2, 1, 8, 128), vm(2, 2, 3, 24, 128),
        vm(2, 8, 128), vm(2, 3, 8, 128), vm(2, GX, GY, 8, 128), vm(64, 128),
        dma((3,)), dma((6, 26)), dma((6, 26)), dma((2, 17)), dma((2, 17)),
    ]
    hbm = pl.BlockSpec(memory_space=pl.ANY)
    return pl.pallas_call(
        kernel,
        out_shape=(
            jax.ShapeDtypeStruct(right_side.shape, F32),
            jax.ShapeDtypeStruct((1, 1, 4), F32),
        ),
        in_specs=[hbm, hbm],
        out_specs=(hbm, pl.BlockSpec(memory_space=pltpu.VMEM)),
        scratch_shapes=scratch,
        compiler_params=pltpu.CompilerParams(
            collective_id=0, has_side_effects=True, vmem_limit_bytes=56 * 2**20),
        name="down_leg",
    )(right_side, coefficient)


def solution(mesh):
    placed = (P("gx", "gy", "gz"), P("gx", "gy", "gz"))
    return jax.shard_map(
        local, mesh=mesh, in_specs=placed, out_specs=placed, check_vma=False)
```

```python
import jax
import jax.numpy as jnp
from jax import lax
from jax.experimental import pallas as pl
from jax.experimental.pallas import tpu as pltpu
from jax.sharding import PartitionSpec as P

MESH = pl.DeviceIdType.MESH
F32 = jnp.float32
GX, GY, GZ = 8, 8, 4
HX = 6
RO = 16
LOCAL = ((32, 32, 128), (16, 16, 64), (8, 8, 128))
OFFSETS = [
    (dx, dy, dz) for dz in (0, 1, -1) for dy in (0, 1, -1) for dx in (0, 1, -1)
    if (dx, dy, dz) != (0, 0, 0)
]
OFFSETS.sort(key=lambda o: abs(o[0]) + abs(o[1]) + abs(o[2]))


def lane_ids(rows):
    return lax.broadcasted_iota(jnp.int32, (rows, 128), 1)


def loop(lo, hi, step, body):
    assert (hi - lo) % step == 0
    def run(j, carry):
        body(lo + j * step)
        return carry
    lax.fori_loop(0, (hi - lo) // step, run, 0)


def zshift(values):
    rows = values[0].shape[0]
    down = [pltpu.roll(v, 1, 1) for v in values]
    up = [pltpu.roll(v, 127, 1) for v in values]
    if len(values) == 1:
        return down, up
    lane = lane_ids(rows)
    first, last = lane == 0, lane == 127
    zm = [jnp.where(first, down[1], down[0]), jnp.where(first, down[0], down[1])]
    zp = [jnp.where(last, up[1], up[0]), jnp.where(last, up[0], up[1])]
    return zm, zp


def coef_pass(K, work, cs, kcs, lo, hi, r0, r1, chunk, unroll, line=False):
    A, Q, D = work["A"], work["Q"], work["D"]
    lane = lane_ids(chunk)
    first, last = lane == 0, lane == 127

    def body(i0):
        for i in [i0 + u for u in range(unroll)]:
            for r in range(r0, r1, chunk):
                rows = pl.ds(r, chunk)
                ks = [K[i, kc, rows, :] for kc in kcs]
                zm, zp = zshift(ks)
                if line:
                    zm = [jnp.where(first, 0.0, v) for v in zm]
                    zp = [jnp.where(last, 0.0, v) for v in zp]
                for n, (c, kc) in enumerate(zip(cs, kcs)):
                    k = ks[n]
                    g = [
                        k + K[i + 1, kc, rows, :],
                        k + K[i - 1, kc, rows, :],
                        k + K[i, kc, pl.ds(r + 1, chunk), :],
                        k + K[i, kc, pl.ds(r - 1, chunk), :],
                        k + zp[n],
                        k + zm[n],
                    ]
                    total = (g[0] + g[1]) + (g[2] + g[3]) + (g[4] + g[5])
                    inside = k > 0.0
                    q = jnp.where(inside, 0.8 / total, 0.0)
                    parts = [q * face for face in g]
                    if line:
                        parts[4] = jnp.where(last, 0.0, parts[4])
                        parts[5] = jnp.where(first, 0.0, parts[5])
                    for j in range(6):
                        A[j, i, c, rows, :] = parts[j]
                    Q[i, c, rows, :] = 2.0 * q
                    D[i, c, rows, :] = jnp.where(inside, 0.625 * total, 0.0)

    loop(lo, hi, unroll, body)


def first_pass(B, work, cs, kcs, lo, hi, r0, r1, unroll):
    Q, C = work["Q"], work["C"]
    rows = pl.ds(r0, r1 - r0)

    def body(i0):
        for i in [i0 + u for u in range(unroll)]:
            for c, kc in zip(cs, kcs):
                C[i, c, rows, :] = Q[i, c, rows, :] * B[i, kc, rows, :]

    loop(lo, hi, unroll, body)


def sweep(X, OUT, work, cs, lo, hi, r0, r1, chunk, unroll, resid):
    A, C, D = work["A"], work["C"], work["D"]

    def body(i0):
        for i in [i0 + u for u in range(unroll)]:
            for r in range(r0, r1, chunk):
                rows = pl.ds(r, chunk)
                vs = [X[i, c, rows, :] for c in cs]
                zm, zp = zshift(vs)
                for n, c in enumerate(cs):
                    s = A[0, i, c, rows, :] * X[i + 1, c, rows, :]
                    s = s + A[1, i, c, rows, :] * X[i - 1, c, rows, :]
                    t = A[2, i, c, rows, :] * X[i, c, pl.ds(r + 1, chunk), :]
                    t = t + A[3, i, c, rows, :] * X[i, c, pl.ds(r - 1, chunk), :]
                    u = A[4, i, c, rows, :] * zp[n] + A[5, i, c, rows, :] * zm[n]
                    total = C[i, c, rows, :] + (s + t) + u
                    if resid:
                        OUT[i, c, rows, :] = D[i, c, rows, :] * (total - 0.8 * vs[n])
                    else:
                        OUT[i, c, rows, :] = total + 0.2 * vs[n]

    loop(lo, hi, unroll, body)


def weights(nz, tile, full):
    lane = lax.broadcasted_iota(jnp.int32, (128, 128), 0)
    coarse = lax.broadcasted_iota(jnp.int32, (128, 128), 1)
    if nz == 128:
        z = lane if tile == 0 else jnp.where(lane < 64, lane + 128, lane - 128)
    else:
        z = jnp.where(lane >= 120, lane - 128, lane)
    delta = z - 2 * coarse
    used = coarse < nz // 2
    inner = used & (delta >= 0) & (delta <= 1)
    if not full:
        return jnp.where(inner, 0.125, 0.0).astype(F32)
    outer = used & ((delta == -1) | (delta == 2))
    return jnp.where(inner, 3.0 / 128.0, jnp.where(outer, 1.0 / 128.0, 0.0)).astype(F32)


def matmul(a, b):
    return jnp.dot(a, b, precision=lax.Precision.HIGHEST, preferred_element_type=F32)


def restrict(R, work, cs, n, base):
    nx, ny, nz = n
    T, S = work["T"], work["S"]
    hy = ny // 2
    lo, size = 8, ny + 16

    def body(I):
        rows = pl.ds(lo, size)
        for c in cs:
            p = base + 2 * I
            T[I, c, rows, :] = (R[p, c, rows, :] + R[p + 3, c, rows, :]) + 3.0 * (
                R[p + 1, c, rows, :] + R[p + 2, c, rows, :])

    loop(0, nx // 2, 1, body)

    def weigh(I, at):
        for m, c in enumerate(cs):
            e = [T[I, c, pl.ds(RO - 1 + j, hy, stride=2), :] for j in range(4)]
            S[m, at, :] = (e[0] + e[3]) + 3.0 * (e[1] + e[2])

    if hy % 8 == 0:
        loop(0, nx // 2, 1, lambda I: weigh(I, pl.ds(pl.multiple_of(I * hy, 8), hy)))
    else:
        for I in range(nx // 2):
            weigh(I, pl.ds(I * hy, hy))
    count = (nx // 2) * hy
    total = matmul(S[0, :count, :], weights(nz, 0, True))
    if len(cs) == 2:
        total = total + matmul(S[1, :count, :], weights(nz, 1, True))
    return total


def coarsen(K, work, n, base):
    nx, ny, nz = n
    T, S = work["T"], work["S"]
    hy = ny // 2
    rows = pl.ds(RO, ny)

    def body(I):
        T[I, 0, rows, :] = K[base + 2 * I, 0, rows, :] + K[base + 2 * I + 1, 0, rows, :]

    loop(0, nx // 2, 1, body)

    def weigh(I, at):
        e = [T[I, 0, pl.ds(RO + j, hy, stride=2), :] for j in range(2)]
        S[0, at, :] = e[0] + e[1]

    if hy % 8 == 0:
        loop(0, nx // 2, 1, lambda I: weigh(I, pl.ds(pl.multiple_of(I * hy, 8), hy)))
    else:
        for I in range(nx // 2):
            weigh(I, pl.ds(I * hy, hy))
    return matmul(S[0, : (nx // 2) * hy, :], weights(nz, 0, False))


def place(dst, value, n, base):
    nx, ny = n[0], n[1]
    for x in range(nx):
        dst[base + x, 0, pl.ds(RO, ny), :] = value[x * ny:(x + 1) * ny, :]


def pack_z(A, pack, n):
    nx, ny, nz = n
    gs = min(16, nx)
    lane = lane_ids(ny)

    def body(g):
        hi = jnp.zeros((ny, 128), F32)
        lo = jnp.zeros((ny, 128), F32)
        for x in range(gs):
            v = A[HX + g * gs + x, 0, pl.ds(RO, ny), :]
            here = (lane >= 8 * x) & (lane < 8 * x + 8)
            hi = jnp.where(here, pltpu.roll(v, (8 * x - nz + 8) % 128, 1), hi)
            lo = jnp.where(here, pltpu.roll(v, 8 * x, 1) if x else v, lo)
        pack[0, g, :, :] = hi
        pack[1, g, :, :] = lo

    loop(0, nx // gs, 1, body)


def unpack_z(A, got, n, keep_lo, keep_hi):
    nx, ny, nz = n
    gs = min(16, nx)
    rows = ny + 16
    lane = lane_ids(rows)
    start = nz % 128
    from_lo = (lane >= 120) & keep_lo
    from_hi = (lane >= start) & (lane < start + 8) & keep_hi

    def body(i):
        xe = i - HX + gs
        g = xe // gs
        at = lax.rem(xe, gs) * 8
        lo = pltpu.roll(got[0, g, :, :], 120 - at, 1)
        hi = pltpu.roll(got[1, g, :, :], lax.rem(start - at + 128, 128), 1)
        if nz == 128:
            own = jnp.zeros((rows, 128), F32)
            A[i, 1, pl.ds(8, rows), :] = jnp.where(from_lo, lo, jnp.where(from_hi, hi, own))
        else:
            own = A[i, 0, pl.ds(8, rows), :]
            A[i, 0, pl.ds(8, rows), :] = jnp.where(from_lo, lo, jnp.where(from_hi, hi, own))

    step = (nx + 2 * HX) // 4
    loop(0, nx + 2 * HX, step, lambda i0: [body(i0 + u) for u in range(step)])


def halo_copies(A, pack, got, ssem, rsem, n, me):
    nx, ny, _ = n
    gs = min(16, nx)
    ng = nx // gs
    xs = {0: (pl.ds(HX, nx), pl.ds(HX, nx)), 1: (pl.ds(nx, HX), pl.ds(0, HX)),
          -1: (pl.ds(HX, HX), pl.ds(nx + HX, HX))}
    ys = {0: (pl.ds(RO, ny), pl.ds(RO, ny)), 1: (pl.ds(RO + ny - 8, 8), pl.ds(8, 8)),
          -1: (pl.ds(RO, 8), pl.ds(RO + ny, 8))}
    gxs = {0: (pl.ds(0, ng), pl.ds(1, ng)), 1: (pl.ds(ng - 1, 1), pl.ds(0, 1)),
           -1: (pl.ds(0, 1), pl.ds(ng + 1, 1))}
    pys = {0: (pl.ds(0, ny), pl.ds(8, ny)), 1: (pl.ds(ny - 8, 8), pl.ds(0, 8)),
           -1: (pl.ds(0, 8), pl.ds(8 + ny, 8))}
    copies = []
    for j, (dx, dy, dz) in enumerate(OFFSETS):
        if dz == 0:
            src = A.at[xs[dx][0], 0, ys[dy][0], :]
            dst = A.at[xs[dx][1], 0, ys[dy][1], :]
        else:
            side = 0 if dz == 1 else 1
            src = pack.at[side, gxs[dx][0], pys[dy][0], :]
            dst = got.at[side, gxs[dx][1], pys[dy][1], :]
        copies.append(pltpu.make_async_remote_copy(
            src_ref=src, dst_ref=dst, send_sem=ssem.at[j], recv_sem=rsem.at[j],
            device_id=peer(me, (dx, dy, dz)), device_id_type=MESH))
    return copies


BLOCKS = [
    (dx, dy, dz) for dz in (2, 1, 3, 0) for dy in (1, -1, 0) for dx in (1, -1, 0)
    if (dx, dy, dz) != (0, 0, 0)
]


def dense_block(rows):
    groups = []
    for g in range(2):
        parts = [rows[32 * g + 8 * j:32 * g + 8 * j + 8, :] for j in range(4)]
        parts = [pltpu.roll(v, 32 * j, 1) if j else v for j, v in enumerate(parts)]
        groups.append((parts[0] + parts[1]) + (parts[2] + parts[3]))
    return groups


def block_copies(N, s, ssem, rsem, me):
    copies = []
    for j, (dx, dy, dz) in enumerate(BLOCKS):
        copies.append(pltpu.make_async_remote_copy(
            src_ref=N.at[s, pl.ds(2, 2), 1, me[2]],
            dst_ref=N.at[s, pl.ds(2 - 2 * dx, 2), 1 - dy, me[2]],
            send_sem=ssem.at[s, j], recv_sem=rsem.at[s, j],
            device_id=peer(me, (dx, dy, dz)), device_id_type=MESH))
    return copies


def assemble(N, s, dst):
    lane = lane_ids(8)

    def body(t):
        for u in range(4):
            j = (u + 2) % 4
            g = t + (u + 2) // 4
            for y in range(3):
                parts = []
                for z in range(GZ):
                    v = N[s, g, y, z, :, :]
                    turn = (32 * (z - j)) % 128
                    parts.append(pltpu.roll(v, turn, 1) if turn else v)
                dst[4 * t + u, 0, pl.ds(8 + 8 * y, 8), :] = jnp.where(
                    lane < 64, jnp.where(lane < 32, parts[0], parts[1]),
                    jnp.where(lane < 96, parts[2], parts[3]))

    for t in range(5):
        body(t)


def peer(me, offset):
    return tuple(lax.rem(m + o + s, s) for m, o, s in zip(me, offset, (GX, GY, GZ)))


def start(copies):
    for copy in copies:
        copy.start()


def clear_outside(K, n, me):
    nx, ny, nz = n
    tiles = 2 if nx == 32 else 1

    def planes(first):
        K[pl.ds(first, HX), :, :, :] = jnp.zeros((HX, tiles, ny + 32, 128), F32)

    def rows(first):
        K[:, :, pl.ds(first, 8), :] = jnp.zeros((nx + 2 * HX, tiles, 8, 128), F32)

    pl.when(me[0] == 0)(lambda: planes(0))
    pl.when(me[0] == GX - 1)(lambda: planes(nx + HX))
    pl.when(me[1] == 0)(lambda: rows(8))
    pl.when(me[1] == GY - 1)(lambda: rows(RO + ny))


def kernel(b_hbm, k_hbm, fine_hbm, out_ref, K0, B0, K1, B1, K2, B2, K3, B3, K4, B4,
           A, Q, D, C, XA, XB, T, S, PS0, PR0, PS1, PR1, N, G, FIN,
           lsem, ssem, rsem, nssem, nrsem, gssem, grsem):
    me = (lax.axis_index("gx"), lax.axis_index("gy"), lax.axis_index("gz"))
    gx, gy, gz = me
    work = {"A": A, "Q": Q, "D": D, "C": C, "T": T, "S": S}
    n0, n1, n2 = LOCAL
    keep_lo, keep_hi = gz > 0, gz < GZ - 1

    own = (pl.ds(HX, 32), 0, pl.ds(RO, 32), slice(None))
    load_k = pltpu.make_async_copy(k_hbm, K0.at[own], lsem.at[0])
    load_b = pltpu.make_async_copy(b_hbm, B0.at[own], lsem.at[1])
    load_k.start()
    load_b.start()

    partners = list(OFFSETS)
    partners += [(d, 0, 0) for d in range(2, GX - 1)]
    partners += [(0, d, 0) for d in range(2, GY - 1)]
    partners += [(dx, dy, 2) for dx in (-1, 0, 1) for dy in (-1, 0, 1)]
    barrier = pltpu.get_barrier_semaphore()
    for offset in partners:
        pl.semaphore_signal(barrier, inc=1, device_id=peer(me, offset), device_id_type=MESH)

    load_k.wait()
    pl.semaphore_wait(barrier, len(partners))
    k0 = halo_copies(K0, PS0.at[0], PR0.at[0], ssem.at[0], rsem.at[0], n0, me)
    b0 = halo_copies(B0, PS0.at[1], PR0.at[1], ssem.at[1], rsem.at[1], n0, me)
    flat = [o[2] == 0 for o in OFFSETS]
    start([c for c, f in zip(k0, flat) if f])
    pack_z(K0, PS0.at[0], n0)
    start([c for c, f in zip(k0, flat) if not f])
    load_b.wait()
    start([c for c, f in zip(b0, flat) if f])
    pack_z(B0, PS0.at[1], n0)
    start([c for c, f in zip(b0, flat) if not f])

    def gather_copies(s):
        y = [pltpu.make_async_remote_copy(
            src_ref=G.at[s, gx, gy], dst_ref=G.at[s, gx, gy], send_sem=gssem.at[s, o - 1],
            recv_sem=grsem.at[s, o - 1], device_id=peer(me, (0, o, 0)), device_id_type=MESH)
            for o in (4, 3, 5, 2, 6, 1, 7)]
        x = [pltpu.make_async_remote_copy(
            src_ref=G.at[s, gx], dst_ref=G.at[s, gx], send_sem=gssem.at[s, 6 + o],
            recv_sem=grsem.at[s, 6 + o], device_id=peer(me, (o, 0, 0)), device_id_type=MESH)
            for o in (4, 3, 5, 2, 6, 1, 7)]
        return y, x

    gk, gb = gather_copies(0), gather_copies(1)

    def gather_y(s, copies, rows):
        G[s, gx, gy, :, :] = rows[:8, :] + pltpu.roll(rows[8:, :], 64, 1)
        start(copies[0])

    def gather_x(copies):
        for copy in copies[0]:
            copy.wait_recv()
        start(copies[1])

    def gather_end(s, copies, dst):
        for copy in copies[1]:
            copy.wait_recv()
        lower = lane_ids(4) < 64

        def body(g):
            for y in range(GY):
                for x in range(4):
                    v = G[s, g, y, pl.ds((x % 2) * 4, 4), :]
                    if x >= 2:
                        v = pltpu.roll(v, 64, 1)
                    dst[1 + 4 * g + x, 0, pl.ds(RO + 4 * y, 4), :] = jnp.where(lower, v, 0.0)

        loop(0, GX, 1, body)
        for group in copies:
            for copy in group:
                copy.wait_send()

    place(K1, coarsen(K0, work, n0, HX), n1, HX)
    pack_z(K1, PS1.at[0], n1)
    k1 = halo_copies(K1, PS1.at[0], PR1.at[0], ssem.at[2], rsem.at[2], n1, me)
    start(k1)
    def send_block(s, rows):
        for g, v in enumerate(dense_block(rows)):
            N[s, 2 + g, 1, gz, :, :] = v
        copies = block_copies(N, s, nssem, nrsem, me)
        start(copies)
        return copies

    def land_block(s, copies, dst):
        for copy in copies:
            copy.wait_recv()
        assemble(N, s, dst)

    k2 = send_block(0, coarsen(K1, work, n1, HX))
    K3[...] = jnp.zeros(K3.shape, F32)
    K4[...] = jnp.zeros(K4.shape, F32)

    def land(copies, dst, got, n, is_k):
        for copy in copies:
            copy.wait_recv()
        for copy in copies:
            copy.wait_send()
        unpack_z(dst, got, n, keep_lo, keep_hi)
        if is_k:
            clear_outside(dst, n, me)

    def coefs(n, K, cs, chunk, step, line=False):
        nx, ny, _ = n
        coef_pass(K, work, cs, cs, 1, nx + 11, 8, ny + 24, chunk, step, line)

    def sweeps(n, B, cs, chunk, steps):
        nx, ny, _ = n
        r0, r1 = 8, ny + 24
        first_pass(B, work, cs, cs, 1, nx + 11, r0, r1, steps[0])
        sweep(C, XA, work, cs, 2, nx + 10, r0, r1, chunk, steps[1], False)
        sweep(XA, XB, work, cs, 2, nx + 10, r0, r1, chunk, steps[1], False)
        sweep(XB, XA, work, cs, 4, nx + 8, r0, r1, chunk, steps[2], False)

    def resid_wide(n, cs, chunk, step):
        nx, ny, _ = n
        sweep(XA, XB, work, cs, 4, nx + 8, 8, ny + 24, chunk, step, True)
        return restrict(XB, work, cs, n, HX - 1)

    land(k0, K0, PR0.at[0], n0, True)
    coefs(n0, K0, (0, 1), 16, 6)
    land(b0, B0, PR0.at[1], n0, False)
    sweeps(n0, B0, (0, 1), 16, (6, 8, 9))
    store = pltpu.make_async_copy(XA.at[own], fine_hbm, lsem.at[2])
    store.start()
    place(B1, resid_wide(n0, (0, 1), 16, 9), n1, HX)
    pack_z(B1, PS1.at[1], n1)
    b1 = halo_copies(B1, PS1.at[1], PR1.at[1], ssem.at[3], rsem.at[3], n1, me)
    start(b1)
    store.wait()
    land(k1, K1, PR1.at[0], n1, True)
    coefs(n1, K1, (0,), 32, 13)
    land_block(0, k2, K2)
    clear_outside(K2, n2, me)
    gather_y(0, gk, coarsen(K2, work, n2, HX))
    land(b1, B1, PR1.at[1], n1, False)
    sweeps(n1, B1, (0,), 32, (13, 8, 10))
    b2 = send_block(1, resid_wide(n1, (0,), 32, 10))
    coefs(n2, K2, (0,), 24, 9, True)
    gather_x(gk)
    land_block(1, b2, B2)
    sweeps(n2, B2, (0,), 24, (9, 8, 6))
    gather_y(1, gb, resid_wide(n2, (0,), 24, 6))
    for copy in k2 + b2:
        copy.wait_send()

    n3, n4 = (32, 32, 64), (16, 16, 32)
    gather_end(0, gk, K3)

    def whole_prepare(n, K, c):
        nx, ny, _ = n
        for X in (C, XA, XB):
            for p in (0, nx + 1):
                X[p, c, pl.ds(8, ny + 16), :] = jnp.zeros((ny + 16, 128), F32)
            for r in (8, RO + ny):
                X[pl.ds(1, nx), c, pl.ds(r, 8), :] = jnp.zeros((nx, 8, 128), F32)
        coef_pass(K, work, (c,), (0,), 1, nx + 1, RO, RO + ny, ny, 16)

    def whole(n, B, c):
        nx, ny, _ = n
        span = (1, nx + 1, RO, RO + ny)
        first_pass(B, work, (c,), (0,), *span, 16)
        sweep(C, XA, work, (c,), *span, ny, 16, False)
        sweep(XA, XB, work, (c,), *span, ny, 16, False)
        sweep(XB, XA, work, (c,), *span, ny, 16, False)
        sweep(XA, XB, work, (c,), *span, ny, 16, True)
        return restrict(XB, work, (c,), n, 0)

    whole_prepare(n3, K3, 0)
    gather_x(gb)
    place(K4, coarsen(K3, work, n3, 1), n4, 1)
    whole_prepare(n4, K4, 1)
    gather_end(1, gb, B3)
    place(B4, whole(n3, B3, 0), n4, 1)
    FIN[...] = whole(n4, B4, 1)
    row = FIN[pl.ds(gx * 8 + gy, 1), :]
    out_ref[0, :, :] = pltpu.roll(row, lax.rem(128 - 4 * gz, 128), 1)[:, :4]


def finish(fine, coarse, fine_out, coarse_out, buf, small, isem, osem):
    loads = [pltpu.make_async_copy(coarse, small, isem.at[4])]
    stores = [pltpu.make_async_copy(small, coarse_out, osem.at[4])]
    for j in range(4):
        part = pl.ds(8 * j, 8)
        loads.append(pltpu.make_async_copy(fine.at[part], buf.at[part], isem.at[j]))
        stores.append(pltpu.make_async_copy(buf.at[part], fine_out.at[part], osem.at[j]))
    start(loads)
    for load, store in zip(loads, stores):
        load.wait()
        store.start()
    for store in stores:
        store.wait()


def local(right_side, coefficient):
    def vm(*shape):
        return pltpu.VMEM(shape, F32)

    dma = pltpu.SemaphoreType.DMA
    scratch = [
        vm(44, 2, 64, 128), vm(44, 2, 64, 128),
        vm(28, 1, 48, 128), vm(28, 1, 48, 128),
        vm(20, 1, 40, 128), vm(20, 1, 40, 128),
        vm(34, 1, 64, 128), vm(34, 1, 64, 128),
        vm(18, 1, 48, 128), vm(18, 1, 48, 128),
        vm(6, 44, 2, 64, 128),
    ] + [vm(44, 2, 64, 128) for _ in range(5)] + [
        vm(16, 2, 64, 128), vm(2, 256, 128),
        vm(2, 2, 2, 32, 128), vm(2, 2, 4, 48, 128),
        vm(2, 2, 1, 16, 128), vm(2, 2, 3, 32, 128),
        vm(2, 6, 3, GZ, 8, 128), vm(2, GX, GY, 8, 128), vm(64, 128),
        dma((3,)), dma((4, 26)), dma((4, 26)), dma((2, 35)), dma((2, 35)), dma((2, 14)), dma((2, 14)),
    ]
    hbm = pl.BlockSpec(memory_space=pl.ANY)
    fine, coarse = pl.pallas_call(
        kernel,
        out_shape=(
            jax.ShapeDtypeStruct(right_side.shape, F32),
            jax.ShapeDtypeStruct((1, 1, 4), F32),
        ),
        in_specs=[hbm, hbm],
        out_specs=(hbm, pl.BlockSpec(memory_space=pltpu.VMEM)),
        scratch_shapes=scratch,
        compiler_params=pltpu.CompilerParams(
            collective_id=0, has_side_effects=True, vmem_limit_bytes=56 * 2**20),
        name="down_leg",
    )(right_side, coefficient)

    return pl.pallas_call(
        finish,
        out_shape=(
            jax.ShapeDtypeStruct(right_side.shape, F32),
            jax.ShapeDtypeStruct((1, 1, 4), F32),
        ),
        in_specs=[hbm, hbm],
        out_specs=(hbm, hbm),
        scratch_shapes=[vm(32, 32, 128), vm(1, 1, 4), dma((5,)), dma((5,))],
        compiler_params=pltpu.CompilerParams(vmem_limit_bytes=60 * 2**20),
        name="finish",
    )(fine, coarse)


def solution(mesh):
    placed = (P("gx", "gy", "gz"), P("gx", "gy", "gz"))
    return jax.shard_map(
        local, mesh=mesh, in_specs=placed, out_specs=placed, check_vma=False)
```

```python
import jax
import jax.numpy as jnp
from jax import lax
from jax.experimental import pallas as pl
from jax.experimental.pallas import tpu as pltpu
from jax.sharding import PartitionSpec as P

MESH = pl.DeviceIdType.MESH
F32 = jnp.float32
GX, GY, GZ = 8, 8, 4
HX = 6
RO = 16
LOCAL = ((32, 32, 128), (16, 16, 64), (8, 8, 128))
OFFSETS = [
    (dx, dy, dz) for dz in (0, 1, -1) for dy in (0, 1, -1) for dx in (0, 1, -1)
    if (dx, dy, dz) != (0, 0, 0)
]
OFFSETS.sort(key=lambda o: abs(o[0]) + abs(o[1]) + abs(o[2]))


def lane_ids(rows):
    return lax.broadcasted_iota(jnp.int32, (rows, 128), 1)


def loop(lo, hi, step, body):
    assert (hi - lo) % step == 0
    def run(j, carry):
        body(lo + j * step)
        return carry
    lax.fori_loop(0, (hi - lo) // step, run, 0)


def zshift(values):
    rows = values[0].shape[0]
    down = [pltpu.roll(v, 1, 1) for v in values]
    up = [pltpu.roll(v, 127, 1) for v in values]
    if len(values) == 1:
        return down, up
    lane = lane_ids(rows)
    first, last = lane == 0, lane == 127
    zm = [jnp.where(first, down[1], down[0]), jnp.where(first, down[0], down[1])]
    zp = [jnp.where(last, up[1], up[0]), jnp.where(last, up[0], up[1])]
    return zm, zp


def coef_pass(K, work, cs, kcs, lo, hi, r0, r1, chunk, unroll, line=False):
    A, Q, D = work["A"], work["Q"], work["D"]
    lane = lane_ids(chunk)
    first, last = lane == 0, lane == 127

    def body(i0):
        for i in [i0 + u for u in range(unroll)]:
            for r in range(r0, r1, chunk):
                rows = pl.ds(r, chunk)
                ks = [K[i, kc, rows, :] for kc in kcs]
                zm, zp = zshift(ks)
                if line:
                    zm = [jnp.where(first, 0.0, v) for v in zm]
                    zp = [jnp.where(last, 0.0, v) for v in zp]
                for n, (c, kc) in enumerate(zip(cs, kcs)):
                    k = ks[n]
                    g = [
                        k + K[i + 1, kc, rows, :],
                        k + K[i - 1, kc, rows, :],
                        k + K[i, kc, pl.ds(r + 1, chunk), :],
                        k + K[i, kc, pl.ds(r - 1, chunk), :],
                        k + zp[n],
                        k + zm[n],
                    ]
                    total = (g[0] + g[1]) + (g[2] + g[3]) + (g[4] + g[5])
                    inside = k > 0.0
                    q = jnp.where(inside, 0.8 / total, 0.0)
                    parts = [q * face for face in g]
                    if line:
                        parts[4] = jnp.where(last, 0.0, parts[4])
                        parts[5] = jnp.where(first, 0.0, parts[5])
                    for j in range(6):
                        A[j, i, c, rows, :] = parts[j]
                    Q[i, c, rows, :] = 2.0 * q
                    D[i, c, rows, :] = jnp.where(inside, 0.625 * total, 0.0)

    loop(lo, hi, unroll, body)


def first_pass(B, work, cs, kcs, lo, hi, r0, r1, unroll):
    Q, C = work["Q"], work["C"]
    rows = pl.ds(r0, r1 - r0)

    def body(i0):
        for i in [i0 + u for u in range(unroll)]:
            for c, kc in zip(cs, kcs):
                C[i, c, rows, :] = Q[i, c, rows, :] * B[i, kc, rows, :]

    loop(lo, hi, unroll, body)


def sweep(X, OUT, work, cs, lo, hi, r0, r1, chunk, unroll, resid):
    A, C, D = work["A"], work["C"], work["D"]

    def body(i0):
        for i in [i0 + u for u in range(unroll)]:
            for r in range(r0, r1, chunk):
                rows = pl.ds(r, chunk)
                vs = [X[i, c, rows, :] for c in cs]
                zm, zp = zshift(vs)
                for n, c in enumerate(cs):
                    s = A[0, i, c, rows, :] * X[i + 1, c, rows, :]
                    s = s + A[1, i, c, rows, :] * X[i - 1, c, rows, :]
                    t = A[2, i, c, rows, :] * X[i, c, pl.ds(r + 1, chunk), :]
                    t = t + A[3, i, c, rows, :] * X[i, c, pl.ds(r - 1, chunk), :]
                    u = A[4, i, c, rows, :] * zp[n] + A[5, i, c, rows, :] * zm[n]
                    total = C[i, c, rows, :] + (s + t) + u
                    if resid:
                        OUT[i, c, rows, :] = D[i, c, rows, :] * (total - 0.8 * vs[n])
                    else:
                        OUT[i, c, rows, :] = total + 0.2 * vs[n]

    loop(lo, hi, unroll, body)


def weights(nz, tile, full):
    lane = lax.broadcasted_iota(jnp.int32, (128, 128), 0)
    coarse = lax.broadcasted_iota(jnp.int32, (128, 128), 1)
    if nz == 128:
        z = lane if tile == 0 else jnp.where(lane < 64, lane + 128, lane - 128)
    else:
        z = jnp.where(lane >= 120, lane - 128, lane)
    delta = z - 2 * coarse
    used = coarse < nz // 2
    inner = used & (delta >= 0) & (delta <= 1)
    if not full:
        return jnp.where(inner, 0.125, 0.0).astype(F32)
    outer = used & ((delta == -1) | (delta == 2))
    return jnp.where(inner, 3.0 / 128.0, jnp.where(outer, 1.0 / 128.0, 0.0)).astype(F32)


def matmul(a, b):
    return jnp.dot(a, b, precision=lax.Precision.HIGHEST, preferred_element_type=F32)


def restrict(R, work, cs, n, base):
    nx, ny, nz = n
    T, S = work["T"], work["S"]
    hy = ny // 2
    lo, size = 8, ny + 16

    def body(I):
        rows = pl.ds(lo, size)
        for c in cs:
            p = base + 2 * I
            T[I, c, rows, :] = (R[p, c, rows, :] + R[p + 3, c, rows, :]) + 3.0 * (
                R[p + 1, c, rows, :] + R[p + 2, c, rows, :])

    loop(0, nx // 2, 4, lambda i0: [body(i0 + u) for u in range(4)])

    def weigh(I, at):
        for m, c in enumerate(cs):
            e = [T[I, c, pl.ds(RO - 1 + j, hy, stride=2), :] for j in range(4)]
            S[m, at, :] = (e[0] + e[3]) + 3.0 * (e[1] + e[2])

    if hy % 8 == 0:
        loop(0, nx // 2, 4, lambda i0: [
            weigh(i0 + u, pl.ds(pl.multiple_of((i0 + u) * hy, 8), hy)) for u in range(4)])
    else:
        for I in range(nx // 2):
            weigh(I, pl.ds(I * hy, hy))
    count = (nx // 2) * hy
    total = matmul(S[0, :count, :], weights(nz, 0, True))
    if len(cs) == 2:
        total = total + matmul(S[1, :count, :], weights(nz, 1, True))
    return total


def coarsen(K, work, n, base):
    nx, ny, nz = n
    T, S = work["T"], work["S"]
    hy = ny // 2
    rows = pl.ds(RO, ny)

    def body(I):
        T[I, 0, rows, :] = K[base + 2 * I, 0, rows, :] + K[base + 2 * I + 1, 0, rows, :]

    loop(0, nx // 2, 4, lambda i0: [body(i0 + u) for u in range(4)])

    def weigh(I, at):
        e = [T[I, 0, pl.ds(RO + j, hy, stride=2), :] for j in range(2)]
        S[0, at, :] = e[0] + e[1]

    if hy % 8 == 0:
        loop(0, nx // 2, 4, lambda i0: [
            weigh(i0 + u, pl.ds(pl.multiple_of((i0 + u) * hy, 8), hy)) for u in range(4)])
    else:
        for I in range(nx // 2):
            weigh(I, pl.ds(I * hy, hy))
    return matmul(S[0, : (nx // 2) * hy, :], weights(nz, 0, False))


def place(dst, value, n, base):
    nx, ny = n[0], n[1]
    for x in range(nx):
        dst[base + x, 0, pl.ds(RO, ny), :] = value[x * ny:(x + 1) * ny, :]


def pack_z(A, pack, n):
    nx, ny, nz = n
    gs = min(16, nx)
    lane = lane_ids(ny)

    def body(g):
        hi = jnp.zeros((ny, 128), F32)
        lo = jnp.zeros((ny, 128), F32)
        for x in range(gs):
            v = A[HX + g * gs + x, 0, pl.ds(RO, ny), :]
            here = (lane >= 8 * x) & (lane < 8 * x + 8)
            hi = jnp.where(here, pltpu.roll(v, (8 * x - nz + 8) % 128, 1), hi)
            lo = jnp.where(here, pltpu.roll(v, 8 * x, 1) if x else v, lo)
        pack[0, g, :, :] = hi
        pack[1, g, :, :] = lo

    loop(0, nx // gs, 1, body)


def unpack_z(A, got, n, keep_lo, keep_hi):
    nx, ny, nz = n
    gs = min(16, nx)
    rows = ny + 16
    lane = lane_ids(rows)
    start = nz % 128
    from_lo = (lane >= 120) & keep_lo
    from_hi = (lane >= start) & (lane < start + 8) & keep_hi

    def body(i):
        xe = i - HX + gs
        g = xe // gs
        at = lax.rem(xe, gs) * 8
        lo = pltpu.roll(got[0, g, :, :], 120 - at, 1)
        hi = pltpu.roll(got[1, g, :, :], lax.rem(start - at + 128, 128), 1)
        if nz == 128:
            own = jnp.zeros((rows, 128), F32)
            A[i, 1, pl.ds(8, rows), :] = jnp.where(from_lo, lo, jnp.where(from_hi, hi, own))
        else:
            own = A[i, 0, pl.ds(8, rows), :]
            A[i, 0, pl.ds(8, rows), :] = jnp.where(from_lo, lo, jnp.where(from_hi, hi, own))

    step = (nx + 2 * HX) // 4
    loop(0, nx + 2 * HX, step, lambda i0: [body(i0 + u) for u in range(step)])


def halo_copies(A, pack, got, ssem, rsem, n, me):
    nx, ny, _ = n
    gs = min(16, nx)
    ng = nx // gs
    xs = {0: (pl.ds(HX, nx), pl.ds(HX, nx)), 1: (pl.ds(nx, HX), pl.ds(0, HX)),
          -1: (pl.ds(HX, HX), pl.ds(nx + HX, HX))}
    ys = {0: (pl.ds(RO, ny), pl.ds(RO, ny)), 1: (pl.ds(RO + ny - 8, 8), pl.ds(8, 8)),
          -1: (pl.ds(RO, 8), pl.ds(RO + ny, 8))}
    gxs = {0: (pl.ds(0, ng), pl.ds(1, ng)), 1: (pl.ds(ng - 1, 1), pl.ds(0, 1)),
           -1: (pl.ds(0, 1), pl.ds(ng + 1, 1))}
    pys = {0: (pl.ds(0, ny), pl.ds(8, ny)), 1: (pl.ds(ny - 8, 8), pl.ds(0, 8)),
           -1: (pl.ds(0, 8), pl.ds(8 + ny, 8))}
    copies = []
    for j, (dx, dy, dz) in enumerate(OFFSETS):
        if dz == 0:
            src = A.at[xs[dx][0], 0, ys[dy][0], :]
            dst = A.at[xs[dx][1], 0, ys[dy][1], :]
        else:
            side = 0 if dz == 1 else 1
            src = pack.at[side, gxs[dx][0], pys[dy][0], :]
            dst = got.at[side, gxs[dx][1], pys[dy][1], :]
        copies.append(pltpu.make_async_remote_copy(
            src_ref=src, dst_ref=dst, send_sem=ssem.at[j], recv_sem=rsem.at[j],
            device_id=peer(me, (dx, dy, dz)), device_id_type=MESH))
    return copies


BLOCKS = [
    (dx, dy, dz) for dz in (2, 1, 3, 0) for dy in (1, -1, 0) for dx in (1, -1, 0)
    if (dx, dy, dz) != (0, 0, 0)
]


def dense_block(rows):
    groups = []
    for g in range(2):
        parts = [rows[32 * g + 8 * j:32 * g + 8 * j + 8, :] for j in range(4)]
        parts = [pltpu.roll(v, 32 * j, 1) if j else v for j, v in enumerate(parts)]
        groups.append((parts[0] + parts[1]) + (parts[2] + parts[3]))
    return groups


def block_copies(N, s, ssem, rsem, me):
    copies = []
    for j, (dx, dy, dz) in enumerate(BLOCKS):
        copies.append(pltpu.make_async_remote_copy(
            src_ref=N.at[s, pl.ds(2, 2), 1, me[2]],
            dst_ref=N.at[s, pl.ds(2 - 2 * dx, 2), 1 - dy, me[2]],
            send_sem=ssem.at[s, j], recv_sem=rsem.at[s, j],
            device_id=peer(me, (dx, dy, dz)), device_id_type=MESH))
    return copies


def assemble(N, s, dst):
    lane = lane_ids(8)

    def body(t):
        for u in range(4):
            j = (u + 2) % 4
            g = t + (u + 2) // 4
            for y in range(3):
                parts = []
                for z in range(GZ):
                    v = N[s, g, y, z, :, :]
                    turn = (32 * (z - j)) % 128
                    parts.append(pltpu.roll(v, turn, 1) if turn else v)
                dst[4 * t + u, 0, pl.ds(8 + 8 * y, 8), :] = jnp.where(
                    lane < 64, jnp.where(lane < 32, parts[0], parts[1]),
                    jnp.where(lane < 96, parts[2], parts[3]))

    for t in range(5):
        body(t)


def peer(me, offset):
    return tuple(lax.rem(m + o + s, s) for m, o, s in zip(me, offset, (GX, GY, GZ)))


def start(copies):
    for copy in copies:
        copy.start()


def clear_outside(K, n, me):
    nx, ny, nz = n
    tiles = 2 if nx == 32 else 1

    def planes(first):
        K[pl.ds(first, HX), :, :, :] = jnp.zeros((HX, tiles, ny + 32, 128), F32)

    def rows(first):
        K[:, :, pl.ds(first, 8), :] = jnp.zeros((nx + 2 * HX, tiles, 8, 128), F32)

    pl.when(me[0] == 0)(lambda: planes(0))
    pl.when(me[0] == GX - 1)(lambda: planes(nx + HX))
    pl.when(me[1] == 0)(lambda: rows(8))
    pl.when(me[1] == GY - 1)(lambda: rows(RO + ny))


def kernel(b_hbm, k_hbm, fine_hbm, out_ref, K0, B0, K1, B1, K2, B2, K3, B3, K4, B4,
           A, Q, D, C, XA, XB, T, S, PS0, PR0, PS1, PR1, N, G, FIN,
           lsem, ssem, rsem, nssem, nrsem, gssem, grsem):
    me = (lax.axis_index("gx"), lax.axis_index("gy"), lax.axis_index("gz"))
    gx, gy, gz = me
    work = {"A": A, "Q": Q, "D": D, "C": C, "T": T, "S": S}
    n0, n1, n2 = LOCAL
    keep_lo, keep_hi = gz > 0, gz < GZ - 1

    own = (pl.ds(HX, 32), 0, pl.ds(RO, 32), slice(None))
    load_k = pltpu.make_async_copy(k_hbm, K0.at[own], lsem.at[0])
    load_b = pltpu.make_async_copy(b_hbm, B0.at[own], lsem.at[1])
    load_k.start()
    load_b.start()

    partners = list(OFFSETS)
    partners += [(d, 0, 0) for d in range(2, GX - 1)]
    partners += [(0, d, 0) for d in range(2, GY - 1)]
    partners += [(dx, dy, 2) for dx in (-1, 0, 1) for dy in (-1, 0, 1)]
    barrier = pltpu.get_barrier_semaphore()
    for offset in partners:
        pl.semaphore_signal(barrier, inc=1, device_id=peer(me, offset), device_id_type=MESH)

    load_k.wait()
    pl.semaphore_wait(barrier, len(partners))
    k0 = halo_copies(K0, PS0.at[0], PR0.at[0], ssem.at[0], rsem.at[0], n0, me)
    b0 = halo_copies(B0, PS0.at[1], PR0.at[1], ssem.at[1], rsem.at[1], n0, me)
    flat = [o[2] == 0 for o in OFFSETS]
    start([c for c, f in zip(k0, flat) if f])
    pack_z(K0, PS0.at[0], n0)
    start([c for c, f in zip(k0, flat) if not f])
    load_b.wait()
    start([c for c, f in zip(b0, flat) if f])
    pack_z(B0, PS0.at[1], n0)
    start([c for c, f in zip(b0, flat) if not f])

    def gather_copies(s):
        y = [pltpu.make_async_remote_copy(
            src_ref=G.at[s, gx, gy], dst_ref=G.at[s, gx, gy], send_sem=gssem.at[s, o - 1],
            recv_sem=grsem.at[s, o - 1], device_id=peer(me, (0, o, 0)), device_id_type=MESH)
            for o in (4, 3, 5, 2, 6, 1, 7)]
        x = [pltpu.make_async_remote_copy(
            src_ref=G.at[s, gx], dst_ref=G.at[s, gx], send_sem=gssem.at[s, 6 + o],
            recv_sem=grsem.at[s, 6 + o], device_id=peer(me, (o, 0, 0)), device_id_type=MESH)
            for o in (4, 3, 5, 2, 6, 1, 7)]
        return y, x

    gk, gb = gather_copies(0), gather_copies(1)

    def gather_y(s, copies, rows):
        G[s, gx, gy, :, :] = rows[:8, :] + pltpu.roll(rows[8:, :], 64, 1)
        start(copies[0])

    def gather_x(copies):
        for copy in copies[0]:
            copy.wait_recv()
        start(copies[1])

    def gather_end(s, copies, dst):
        for copy in copies[1]:
            copy.wait_recv()
        lower = lane_ids(8) < 64
        top = lax.broadcasted_iota(jnp.int32, (8, 128), 0) < 4

        def body(g):
            for m in range(GY // 2):
                a, b = G[s, g, 2 * m, :, :], G[s, g, 2 * m + 1, :, :]
                first = jnp.where(top, a, pltpu.roll(b, 4, 0))
                second = jnp.where(top, pltpu.roll(a, 4, 0), b)
                planes = (first, second, pltpu.roll(first, 64, 1), pltpu.roll(second, 64, 1))
                for p, v in enumerate(planes):
                    dst[1 + 4 * g + p, 0, pl.ds(RO + 8 * m, 8), :] = jnp.where(lower, v, 0.0)

        loop(0, GX, 2, lambda g: (body(g), body(g + 1)))
        for group in copies:
            for copy in group:
                copy.wait_send()

    place(K1, coarsen(K0, work, n0, HX), n1, HX)
    pack_z(K1, PS1.at[0], n1)
    k1 = halo_copies(K1, PS1.at[0], PR1.at[0], ssem.at[2], rsem.at[2], n1, me)
    start(k1)
    def send_block(s, rows):
        for g, v in enumerate(dense_block(rows)):
            N[s, 2 + g, 1, gz, :, :] = v
        copies = block_copies(N, s, nssem, nrsem, me)
        start(copies)
        return copies

    def land_block(s, copies, dst):
        for copy in copies:
            copy.wait_recv()
        assemble(N, s, dst)

    k2 = send_block(0, coarsen(K1, work, n1, HX))
    K3[...] = jnp.zeros(K3.shape, F32)
    K4[...] = jnp.zeros(K4.shape, F32)

    def land(copies, dst, got, n, is_k):
        for copy in copies:
            copy.wait_recv()
        for copy in copies:
            copy.wait_send()
        unpack_z(dst, got, n, keep_lo, keep_hi)
        if is_k:
            clear_outside(dst, n, me)

    def coefs(n, K, cs, chunk, step, line=False):
        nx, ny, _ = n
        coef_pass(K, work, cs, cs, 1, nx + 11, 8, ny + 24, chunk, step, line)

    def sweeps(n, B, cs, chunk, steps):
        nx, ny, _ = n
        r0, r1 = 8, ny + 24
        first_pass(B, work, cs, cs, 1, nx + 11, r0, r1, steps[0])
        sweep(C, XA, work, cs, 2, nx + 10, r0, r1, chunk, steps[1], False)
        sweep(XA, XB, work, cs, 2, nx + 10, r0, r1, chunk, steps[1], False)
        sweep(XB, XA, work, cs, 4, nx + 8, r0, r1, chunk, steps[2], False)

    def resid_wide(n, cs, chunk, step):
        nx, ny, _ = n
        sweep(XA, XB, work, cs, 5, nx + 7, 8, ny + 24, chunk, step, True)
        return restrict(XB, work, cs, n, HX - 1)

    land(k0, K0, PR0.at[0], n0, True)
    coefs(n0, K0, (0, 1), 16, 6)
    land(b0, B0, PR0.at[1], n0, False)
    sweeps(n0, B0, (0, 1), 16, (6, 10, 18))
    store = pltpu.make_async_copy(XA.at[own], fine_hbm, lsem.at[2])
    store.start()
    place(B1, resid_wide(n0, (0, 1), 16, 17), n1, HX)
    pack_z(B1, PS1.at[1], n1)
    b1 = halo_copies(B1, PS1.at[1], PR1.at[1], ssem.at[3], rsem.at[3], n1, me)
    start(b1)
    store.wait()
    land(k1, K1, PR1.at[0], n1, True)
    coefs(n1, K1, (0,), 32, 13)
    land_block(0, k2, K2)
    clear_outside(K2, n2, me)
    gather_y(0, gk, coarsen(K2, work, n2, HX))
    land(b1, B1, PR1.at[1], n1, False)
    sweeps(n1, B1, (0,), 32, (13, 12, 10))
    b2 = send_block(1, resid_wide(n1, (0,), 32, 9))
    coefs(n2, K2, (0,), 24, 9, True)
    gather_x(gk)
    land_block(1, b2, B2)
    sweeps(n2, B2, (0,), 24, (9, 8, 6))
    gather_y(1, gb, resid_wide(n2, (0,), 24, 5))
    for copy in k2 + b2:
        copy.wait_send()

    n3, n4 = (32, 32, 64), (16, 16, 32)
    gather_end(0, gk, K3)

    def whole_prepare(n, K, c):
        nx, ny, _ = n
        for X in (C, XA, XB):
            for p in (0, nx + 1):
                X[p, c, pl.ds(8, ny + 16), :] = jnp.zeros((ny + 16, 128), F32)
            for r in (8, RO + ny):
                X[pl.ds(1, nx), c, pl.ds(r, 8), :] = jnp.zeros((nx, 8, 128), F32)
        coef_pass(K, work, (c,), (0,), 1, nx + 1, RO, RO + ny, ny, 16)

    def whole(n, B, c):
        nx, ny, _ = n
        span = (1, nx + 1, RO, RO + ny)
        first_pass(B, work, (c,), (0,), *span, 16)
        sweep(C, XA, work, (c,), *span, ny, 16, False)
        sweep(XA, XB, work, (c,), *span, ny, 16, False)
        sweep(XB, XA, work, (c,), *span, ny, 16, False)
        sweep(XA, XB, work, (c,), *span, ny, 16, True)
        return restrict(XB, work, (c,), n, 0)

    whole_prepare(n3, K3, 0)
    gather_x(gb)
    place(K4, coarsen(K3, work, n3, 1), n4, 1)
    whole_prepare(n4, K4, 1)
    gather_end(1, gb, B3)
    place(B4, whole(n3, B3, 0), n4, 1)
    FIN[...] = whole(n4, B4, 1)
    row = FIN[pl.ds(gx * 8 + gy, 1), :]
    out_ref[0, :, :] = pltpu.roll(row, lax.rem(128 - 4 * gz, 128), 1)[:, :4]


def finish(fine, coarse, fine_out, coarse_out, buf, small, isem, osem):
    loads = [pltpu.make_async_copy(coarse, small, isem.at[4])]
    stores = [pltpu.make_async_copy(small, coarse_out, osem.at[4])]
    for j in range(4):
        part = pl.ds(8 * j, 8)
        loads.append(pltpu.make_async_copy(fine.at[part], buf.at[part], isem.at[j]))
        stores.append(pltpu.make_async_copy(buf.at[part], fine_out.at[part], osem.at[j]))
    start(loads)
    for load, store in zip(loads, stores):
        load.wait()
        store.start()
    for store in stores:
        store.wait()


def local(right_side, coefficient):
    def vm(*shape):
        return pltpu.VMEM(shape, F32)

    dma = pltpu.SemaphoreType.DMA
    scratch = [
        vm(44, 2, 64, 128), vm(44, 2, 64, 128),
        vm(28, 1, 48, 128), vm(28, 1, 48, 128),
        vm(20, 1, 40, 128), vm(20, 1, 40, 128),
        vm(34, 1, 64, 128), vm(34, 1, 64, 128),
        vm(18, 1, 48, 128), vm(18, 1, 48, 128),
        vm(6, 44, 2, 64, 128),
    ] + [vm(44, 2, 64, 128) for _ in range(5)] + [
        vm(16, 2, 64, 128), vm(2, 256, 128),
        vm(2, 2, 2, 32, 128), vm(2, 2, 4, 48, 128),
        vm(2, 2, 1, 16, 128), vm(2, 2, 3, 32, 128),
        vm(2, 6, 3, GZ, 8, 128), vm(2, GX, GY, 8, 128), vm(64, 128),
        dma((3,)), dma((4, 26)), dma((4, 26)), dma((2, 35)), dma((2, 35)), dma((2, 14)), dma((2, 14)),
    ]
    hbm = pl.BlockSpec(memory_space=pl.ANY)
    fine, coarse = pl.pallas_call(
        kernel,
        out_shape=(
            jax.ShapeDtypeStruct(right_side.shape, F32),
            jax.ShapeDtypeStruct((1, 1, 4), F32),
        ),
        in_specs=[hbm, hbm],
        out_specs=(hbm, pl.BlockSpec(memory_space=pltpu.VMEM)),
        scratch_shapes=scratch,
        compiler_params=pltpu.CompilerParams(
            collective_id=0, has_side_effects=True, vmem_limit_bytes=56 * 2**20),
        name="down_leg",
    )(right_side, coefficient)

    return pl.pallas_call(
        finish,
        out_shape=(
            jax.ShapeDtypeStruct(right_side.shape, F32),
            jax.ShapeDtypeStruct((1, 1, 4), F32),
        ),
        in_specs=[hbm, hbm],
        out_specs=(hbm, hbm),
        scratch_shapes=[vm(32, 32, 128), vm(1, 1, 4), dma((5,)), dma((5,))],
        compiler_params=pltpu.CompilerParams(vmem_limit_bytes=60 * 2**20),
        name="finish",
    )(fine, coarse)


def solution(mesh):
    placed = (P("gx", "gy", "gz"), P("gx", "gy", "gz"))
    return jax.shard_map(
        local, mesh=mesh, in_specs=placed, out_specs=placed, check_vma=False)
```

```python
import jax
import jax.numpy as jnp
from jax import lax
from jax.experimental import pallas as pl
from jax.experimental.pallas import tpu as pltpu
from jax.sharding import PartitionSpec as P

MESH = pl.DeviceIdType.MESH
F32 = jnp.float32
GX, GY, GZ = 8, 8, 4
HX = 6
RO = 16
LOCAL = ((32, 32, 128), (16, 16, 64), (8, 8, 128))
OFFSETS = [
    (dx, dy, dz) for dz in (0, 1, -1) for dy in (0, 1, -1) for dx in (0, 1, -1)
    if (dx, dy, dz) != (0, 0, 0)
]
OFFSETS.sort(key=lambda o: abs(o[0]) + abs(o[1]) + abs(o[2]))


def lane_ids(rows):
    return lax.broadcasted_iota(jnp.int32, (rows, 128), 1)


def loop(lo, hi, step, body):
    assert (hi - lo) % step == 0
    def run(j, carry):
        body(lo + j * step)
        return carry
    lax.fori_loop(0, (hi - lo) // step, run, 0)


def zshift(values):
    rows = values[0].shape[0]
    down = [pltpu.roll(v, 1, 1) for v in values]
    up = [pltpu.roll(v, 127, 1) for v in values]
    if len(values) == 1:
        return down, up
    lane = lane_ids(rows)
    first, last = lane == 0, lane == 127
    zm = [jnp.where(first, down[1], down[0]), jnp.where(first, down[0], down[1])]
    zp = [jnp.where(last, up[1], up[0]), jnp.where(last, up[0], up[1])]
    return zm, zp


def coef_pass(K, work, cs, kcs, lo, hi, r0, r1, chunk, unroll, line=False):
    A, Q, D = work["A"], work["Q"], work["D"]
    lane = lane_ids(chunk)
    first, last = lane == 0, lane == 127

    def body(i0):
        for i in [i0 + u for u in range(unroll)]:
            for r in range(r0, r1, chunk):
                rows = pl.ds(r, chunk)
                ks = [K[i, kc, rows, :] for kc in kcs]
                zm, zp = zshift(ks)
                if line:
                    zm = [jnp.where(first, 0.0, v) for v in zm]
                    zp = [jnp.where(last, 0.0, v) for v in zp]
                for n, (c, kc) in enumerate(zip(cs, kcs)):
                    k = ks[n]
                    g = [
                        k + K[i + 1, kc, rows, :],
                        k + K[i - 1, kc, rows, :],
                        k + K[i, kc, pl.ds(r + 1, chunk), :],
                        k + K[i, kc, pl.ds(r - 1, chunk), :],
                        k + zp[n],
                        k + zm[n],
                    ]
                    total = (g[0] + g[1]) + (g[2] + g[3]) + (g[4] + g[5])
                    inside = k > 0.0
                    q = jnp.where(inside, 0.8 / total, 0.0)
                    parts = [q * face for face in g]
                    if line:
                        parts[4] = jnp.where(last, 0.0, parts[4])
                        parts[5] = jnp.where(first, 0.0, parts[5])
                    for j in range(6):
                        A[j, i, c, rows, :] = parts[j]
                    Q[i, c, rows, :] = 2.0 * q
                    D[i, c, rows, :] = jnp.where(inside, 0.625 * total, 0.0)

    loop(lo, hi, unroll, body)


def first_pass(B, work, cs, kcs, lo, hi, r0, r1, unroll):
    Q, C = work["Q"], work["C"]
    rows = pl.ds(r0, r1 - r0)

    def body(i0):
        for i in [i0 + u for u in range(unroll)]:
            for c, kc in zip(cs, kcs):
                C[i, c, rows, :] = Q[i, c, rows, :] * B[i, kc, rows, :]

    loop(lo, hi, unroll, body)


def sweep(X, OUT, work, cs, lo, hi, r0, r1, chunk, unroll, resid):
    A, C, D = work["A"], work["C"], work["D"]

    def body(i0):
        for i in [i0 + u for u in range(unroll)]:
            for r in range(r0, r1, chunk):
                rows = pl.ds(r, chunk)
                vs = [X[i, c, rows, :] for c in cs]
                zm, zp = zshift(vs)
                for n, c in enumerate(cs):
                    s = A[0, i, c, rows, :] * X[i + 1, c, rows, :]
                    s = s + A[1, i, c, rows, :] * X[i - 1, c, rows, :]
                    t = A[2, i, c, rows, :] * X[i, c, pl.ds(r + 1, chunk), :]
                    t = t + A[3, i, c, rows, :] * X[i, c, pl.ds(r - 1, chunk), :]
                    u = A[4, i, c, rows, :] * zp[n] + A[5, i, c, rows, :] * zm[n]
                    total = C[i, c, rows, :] + (s + t) + u
                    if resid:
                        OUT[i, c, rows, :] = D[i, c, rows, :] * (total - 0.8 * vs[n])
                    else:
                        OUT[i, c, rows, :] = total + 0.2 * vs[n]

    loop(lo, hi, unroll, body)


def weights(nz, tile, full):
    lane = lax.broadcasted_iota(jnp.int32, (128, 128), 0)
    coarse = lax.broadcasted_iota(jnp.int32, (128, 128), 1)
    if nz == 128:
        z = lane if tile == 0 else jnp.where(lane < 64, lane + 128, lane - 128)
    else:
        z = jnp.where(lane >= 120, lane - 128, lane)
    delta = z - 2 * coarse
    used = coarse < nz // 2
    inner = used & (delta >= 0) & (delta <= 1)
    if not full:
        return jnp.where(inner, 0.125, 0.0).astype(F32)
    outer = used & ((delta == -1) | (delta == 2))
    return jnp.where(inner, 3.0 / 128.0, jnp.where(outer, 1.0 / 128.0, 0.0)).astype(F32)


def matmul(a, b):
    return jnp.dot(a, b, precision=lax.Precision.HIGHEST, preferred_element_type=F32)


def restrict(R, work, cs, n, base):
    nx, ny, nz = n
    T, S = work["T"], work["S"]
    hy = ny // 2
    lo, size = 8, ny + 16

    def body(I):
        rows = pl.ds(lo, size)
        for c in cs:
            p = base + 2 * I
            T[I, c, rows, :] = (R[p, c, rows, :] + R[p + 3, c, rows, :]) + 3.0 * (
                R[p + 1, c, rows, :] + R[p + 2, c, rows, :])

    loop(0, nx // 2, 4, lambda i0: [body(i0 + u) for u in range(4)])

    def weigh(I, at):
        for m, c in enumerate(cs):
            e = [T[I, c, pl.ds(RO - 1 + j, hy, stride=2), :] for j in range(4)]
            S[m, at, :] = (e[0] + e[3]) + 3.0 * (e[1] + e[2])

    if hy % 8 == 0:
        loop(0, nx // 2, 4, lambda i0: [
            weigh(i0 + u, pl.ds(pl.multiple_of((i0 + u) * hy, 8), hy)) for u in range(4)])
    else:
        for I in range(nx // 2):
            weigh(I, pl.ds(I * hy, hy))
    count = (nx // 2) * hy
    total = matmul(S[0, :count, :], weights(nz, 0, True))
    if len(cs) == 2:
        total = total + matmul(S[1, :count, :], weights(nz, 1, True))
    return total


def coarsen(K, work, n, base):
    nx, ny, nz = n
    T, S = work["T"], work["S"]
    hy = ny // 2
    rows = pl.ds(RO, ny)

    def body(I):
        T[I, 0, rows, :] = K[base + 2 * I, 0, rows, :] + K[base + 2 * I + 1, 0, rows, :]

    loop(0, nx // 2, 4, lambda i0: [body(i0 + u) for u in range(4)])

    def weigh(I, at):
        e = [T[I, 0, pl.ds(RO + j, hy, stride=2), :] for j in range(2)]
        S[0, at, :] = e[0] + e[1]

    if hy % 8 == 0:
        loop(0, nx // 2, 4, lambda i0: [
            weigh(i0 + u, pl.ds(pl.multiple_of((i0 + u) * hy, 8), hy)) for u in range(4)])
    else:
        for I in range(nx // 2):
            weigh(I, pl.ds(I * hy, hy))
    return matmul(S[0, : (nx // 2) * hy, :], weights(nz, 0, False))


def place(dst, value, n, base):
    nx, ny = n[0], n[1]
    for x in range(nx):
        dst[base + x, 0, pl.ds(RO, ny), :] = value[x * ny:(x + 1) * ny, :]


def pack_z(A, pack, n):
    nx, ny, nz = n
    gs = min(16, nx)
    lane = lane_ids(ny)

    def body(g):
        hi = jnp.zeros((ny, 128), F32)
        lo = jnp.zeros((ny, 128), F32)
        for x in range(gs):
            v = A[HX + g * gs + x, 0, pl.ds(RO, ny), :]
            here = (lane >= 8 * x) & (lane < 8 * x + 8)
            hi = jnp.where(here, pltpu.roll(v, (8 * x - nz + 8) % 128, 1), hi)
            lo = jnp.where(here, pltpu.roll(v, 8 * x, 1) if x else v, lo)
        pack[0, g, :, :] = hi
        pack[1, g, :, :] = lo

    loop(0, nx // gs, 1, body)


def unpack_z(A, got, n, keep_lo, keep_hi):
    nx, ny, nz = n
    gs = min(16, nx)
    rows = ny + 16
    lane = lane_ids(rows)
    start = nz % 128
    from_lo = (lane >= 120) & keep_lo
    from_hi = (lane >= start) & (lane < start + 8) & keep_hi

    def body(i):
        xe = i - HX + gs
        g = xe // gs
        at = lax.rem(xe, gs) * 8
        lo = pltpu.roll(got[0, g, :, :], 120 - at, 1)
        hi = pltpu.roll(got[1, g, :, :], lax.rem(start - at + 128, 128), 1)
        if nz == 128:
            own = jnp.zeros((rows, 128), F32)
            A[i, 1, pl.ds(8, rows), :] = jnp.where(from_lo, lo, jnp.where(from_hi, hi, own))
        else:
            own = A[i, 0, pl.ds(8, rows), :]
            A[i, 0, pl.ds(8, rows), :] = jnp.where(from_lo, lo, jnp.where(from_hi, hi, own))

    step = (nx + 2 * HX) // 4
    loop(0, nx + 2 * HX, step, lambda i0: [body(i0 + u) for u in range(step)])


def halo_copies(A, pack, got, ssem, rsem, n, me, w=HX):
    nx, ny, _ = n
    gs = min(16, nx)
    ng = nx // gs
    xs = {0: (pl.ds(HX, nx), pl.ds(HX, nx)), 1: (pl.ds(HX + nx - w, w), pl.ds(HX - w, w)),
          -1: (pl.ds(HX, w), pl.ds(nx + HX, w))}
    ys = {0: (pl.ds(RO, ny), pl.ds(RO, ny)), 1: (pl.ds(RO + ny - 8, 8), pl.ds(8, 8)),
          -1: (pl.ds(RO, 8), pl.ds(RO + ny, 8))}
    gxs = {0: (pl.ds(0, ng), pl.ds(1, ng)), 1: (pl.ds(ng - 1, 1), pl.ds(0, 1)),
           -1: (pl.ds(0, 1), pl.ds(ng + 1, 1))}
    pys = {0: (pl.ds(0, ny), pl.ds(8, ny)), 1: (pl.ds(ny - 8, 8), pl.ds(0, 8)),
           -1: (pl.ds(0, 8), pl.ds(8 + ny, 8))}
    copies = []
    for j, (dx, dy, dz) in enumerate(OFFSETS):
        if dz == 0:
            src = A.at[xs[dx][0], 0, ys[dy][0], :]
            dst = A.at[xs[dx][1], 0, ys[dy][1], :]
        else:
            side = 0 if dz == 1 else 1
            src = pack.at[side, gxs[dx][0], pys[dy][0], :]
            dst = got.at[side, gxs[dx][1], pys[dy][1], :]
        copies.append(pltpu.make_async_remote_copy(
            src_ref=src, dst_ref=dst, send_sem=ssem.at[j], recv_sem=rsem.at[j],
            device_id=peer(me, (dx, dy, dz)), device_id_type=MESH))
    return copies


BLOCKS = [
    (dx, dy, dz) for dz in (2, 1, 3, 0) for dy in (1, -1, 0) for dx in (1, -1, 0)
    if (dx, dy, dz) != (0, 0, 0)
]


def dense_block(rows):
    groups = []
    for g in range(2):
        parts = [rows[32 * g + 8 * j:32 * g + 8 * j + 8, :] for j in range(4)]
        parts = [pltpu.roll(v, 32 * j, 1) if j else v for j, v in enumerate(parts)]
        groups.append((parts[0] + parts[1]) + (parts[2] + parts[3]))
    return groups


def block_copies(N, s, ssem, rsem, me):
    copies = []
    for j, (dx, dy, dz) in enumerate(BLOCKS):
        copies.append(pltpu.make_async_remote_copy(
            src_ref=N.at[s, pl.ds(2, 2), 1, me[2]],
            dst_ref=N.at[s, pl.ds(2 - 2 * dx, 2), 1 - dy, me[2]],
            send_sem=ssem.at[s, j], recv_sem=rsem.at[s, j],
            device_id=peer(me, (dx, dy, dz)), device_id_type=MESH))
    return copies


def assemble(N, s, dst):
    lane = lane_ids(8)

    def body(t):
        for u in range(4):
            j = (u + 2) % 4
            g = t + (u + 2) // 4
            for y in range(3):
                parts = []
                for z in range(GZ):
                    v = N[s, g, y, z, :, :]
                    turn = (32 * (z - j)) % 128
                    parts.append(pltpu.roll(v, turn, 1) if turn else v)
                dst[4 * t + u, 0, pl.ds(8 + 8 * y, 8), :] = jnp.where(
                    lane < 64, jnp.where(lane < 32, parts[0], parts[1]),
                    jnp.where(lane < 96, parts[2], parts[3]))

    for t in range(5):
        body(t)


def peer(me, offset):
    return tuple(lax.rem(m + o + s, s) for m, o, s in zip(me, offset, (GX, GY, GZ)))


def start(copies):
    for copy in copies:
        copy.start()


def clear_outside(K, n, me):
    nx, ny, nz = n
    tiles = 2 if nx == 32 else 1

    def planes(first):
        K[pl.ds(first, HX), :, :, :] = jnp.zeros((HX, tiles, ny + 32, 128), F32)

    def rows(first):
        K[:, :, pl.ds(first, 8), :] = jnp.zeros((nx + 2 * HX, tiles, 8, 128), F32)

    pl.when(me[0] == 0)(lambda: planes(0))
    pl.when(me[0] == GX - 1)(lambda: planes(nx + HX))
    pl.when(me[1] == 0)(lambda: rows(8))
    pl.when(me[1] == GY - 1)(lambda: rows(RO + ny))


def kernel(b_hbm, k_hbm, fine_hbm, out_ref, K0, B0, K1, B1, K2, B2, K3, B3, K4, B4,
           A, Q, D, C, XA, XB, T, S, PS0, PR0, PS1, PR1, N, G, FIN,
           lsem, ssem, rsem, nssem, nrsem, gssem, grsem):
    me = (lax.axis_index("gx"), lax.axis_index("gy"), lax.axis_index("gz"))
    gx, gy, gz = me
    work = {"A": A, "Q": Q, "D": D, "C": C, "T": T, "S": S}
    n0, n1, n2 = LOCAL
    keep_lo, keep_hi = gz > 0, gz < GZ - 1

    own = (pl.ds(HX, 32), 0, pl.ds(RO, 32), slice(None))
    load_k = pltpu.make_async_copy(k_hbm, K0.at[own], lsem.at[0])
    load_b = pltpu.make_async_copy(b_hbm, B0.at[own], lsem.at[1])
    load_k.start()
    load_b.start()

    partners = list(OFFSETS)
    partners += [(d, 0, 0) for d in range(2, GX - 1)]
    partners += [(0, d, 0) for d in range(2, GY - 1)]
    partners += [(dx, dy, 2) for dx in (-1, 0, 1) for dy in (-1, 0, 1)]
    barrier = pltpu.get_barrier_semaphore()
    for offset in partners:
        pl.semaphore_signal(barrier, inc=1, device_id=peer(me, offset), device_id_type=MESH)

    load_k.wait()
    pl.semaphore_wait(barrier, len(partners))
    k0 = halo_copies(K0, PS0.at[0], PR0.at[0], ssem.at[0], rsem.at[0], n0, me)
    b0 = halo_copies(B0, PS0.at[1], PR0.at[1], ssem.at[1], rsem.at[1], n0, me, HX - 1)
    flat = [o[2] == 0 for o in OFFSETS]
    start([c for c, f in zip(k0, flat) if f])
    pack_z(K0, PS0.at[0], n0)
    start([c for c, f in zip(k0, flat) if not f])
    load_b.wait()
    start([c for c, f in zip(b0, flat) if f])
    pack_z(B0, PS0.at[1], n0)
    start([c for c, f in zip(b0, flat) if not f])

    def gather_copies(s):
        y = [pltpu.make_async_remote_copy(
            src_ref=G.at[s, gx, gy], dst_ref=G.at[s, gx, gy], send_sem=gssem.at[s, o - 1],
            recv_sem=grsem.at[s, o - 1], device_id=peer(me, (0, o, 0)), device_id_type=MESH)
            for o in (4, 3, 5, 2, 6, 1, 7)]
        x = [pltpu.make_async_remote_copy(
            src_ref=G.at[s, gx], dst_ref=G.at[s, gx], send_sem=gssem.at[s, 6 + o],
            recv_sem=grsem.at[s, 6 + o], device_id=peer(me, (o, 0, 0)), device_id_type=MESH)
            for o in (4, 3, 5, 2, 6, 1, 7)]
        return y, x

    gk, gb = gather_copies(0), gather_copies(1)

    def gather_y(s, copies, rows):
        G[s, gx, gy, :, :] = rows[:8, :] + pltpu.roll(rows[8:, :], 64, 1)
        start(copies[0])

    def gather_x(copies):
        for copy in copies[0]:
            copy.wait_recv()
        start(copies[1])

    def gather_end(s, copies, dst):
        for copy in copies[1]:
            copy.wait_recv()
        lower = lane_ids(8) < 64
        top = lax.broadcasted_iota(jnp.int32, (8, 128), 0) < 4

        def body(g):
            for m in range(GY // 2):
                a, b = G[s, g, 2 * m, :, :], G[s, g, 2 * m + 1, :, :]
                first = jnp.where(top, a, pltpu.roll(b, 4, 0))
                second = jnp.where(top, pltpu.roll(a, 4, 0), b)
                planes = (first, second, pltpu.roll(first, 64, 1), pltpu.roll(second, 64, 1))
                for p, v in enumerate(planes):
                    dst[1 + 4 * g + p, 0, pl.ds(RO + 8 * m, 8), :] = jnp.where(lower, v, 0.0)

        loop(0, GX, 2, lambda g: (body(g), body(g + 1)))
        for group in copies:
            for copy in group:
                copy.wait_send()

    place(K1, coarsen(K0, work, n0, HX), n1, HX)
    pack_z(K1, PS1.at[0], n1)
    k1 = halo_copies(K1, PS1.at[0], PR1.at[0], ssem.at[2], rsem.at[2], n1, me)
    start(k1)
    def send_block(s, rows):
        for g, v in enumerate(dense_block(rows)):
            N[s, 2 + g, 1, gz, :, :] = v
        copies = block_copies(N, s, nssem, nrsem, me)
        start(copies)
        return copies

    def land_block(s, copies, dst):
        for copy in copies:
            copy.wait_recv()
        assemble(N, s, dst)

    k2 = send_block(0, coarsen(K1, work, n1, HX))
    K3[...] = jnp.zeros(K3.shape, F32)
    K4[...] = jnp.zeros(K4.shape, F32)

    def land(copies, dst, got, n, is_k):
        for copy in copies:
            copy.wait_recv()
        for copy in copies:
            copy.wait_send()
        unpack_z(dst, got, n, keep_lo, keep_hi)
        if is_k:
            clear_outside(dst, n, me)

    def coefs(n, K, cs, chunk, step, line=False):
        nx, ny, _ = n
        coef_pass(K, work, cs, cs, 1, nx + 11, 8, ny + 24, chunk, step, line)

    def sweeps(n, B, cs, chunk, steps):
        nx, ny, _ = n
        r0, r1 = 8, ny + 24
        first_pass(B, work, cs, cs, 1, nx + 11, r0, r1, steps[0])
        sweep(C, XA, work, cs, 2, nx + 10, r0, r1, chunk, steps[1], False)
        sweep(XA, XB, work, cs, 2, nx + 10, r0, r1, chunk, steps[1], False)
        sweep(XB, XA, work, cs, 4, nx + 8, r0, r1, chunk, steps[2], False)

    def resid_wide(n, cs, chunk, step):
        nx, ny, _ = n
        sweep(XA, XB, work, cs, 5, nx + 7, 8, ny + 24, chunk, step, True)
        return restrict(XB, work, cs, n, HX - 1)

    land(k0, K0, PR0.at[0], n0, True)
    coefs(n0, K0, (0, 1), 16, 6)
    land(b0, B0, PR0.at[1], n0, False)
    sweeps(n0, B0, (0, 1), 16, (6, 10, 18))
    store = pltpu.make_async_copy(XA.at[own], fine_hbm, lsem.at[2])
    store.start()
    place(B1, resid_wide(n0, (0, 1), 16, 17), n1, HX)
    pack_z(B1, PS1.at[1], n1)
    b1 = halo_copies(B1, PS1.at[1], PR1.at[1], ssem.at[3], rsem.at[3], n1, me, HX - 1)
    start(b1)
    store.wait()
    land(k1, K1, PR1.at[0], n1, True)
    coefs(n1, K1, (0,), 32, 13)
    land_block(0, k2, K2)
    clear_outside(K2, n2, me)
    gather_y(0, gk, coarsen(K2, work, n2, HX))
    land(b1, B1, PR1.at[1], n1, False)
    sweeps(n1, B1, (0,), 32, (13, 12, 10))
    b2 = send_block(1, resid_wide(n1, (0,), 32, 9))
    coefs(n2, K2, (0,), 24, 9, True)
    gather_x(gk)
    land_block(1, b2, B2)
    sweeps(n2, B2, (0,), 24, (9, 8, 6))
    gather_y(1, gb, resid_wide(n2, (0,), 24, 5))
    for copy in k2 + b2:
        copy.wait_send()

    n3, n4 = (32, 32, 64), (16, 16, 32)
    gather_end(0, gk, K3)

    def whole_prepare(n, K, c):
        nx, ny, _ = n
        for X in (C, XA, XB):
            for p in (0, nx + 1):
                X[p, c, pl.ds(8, ny + 16), :] = jnp.zeros((ny + 16, 128), F32)
            for r in (8, RO + ny):
                X[pl.ds(1, nx), c, pl.ds(r, 8), :] = jnp.zeros((nx, 8, 128), F32)
        coef_pass(K, work, (c,), (0,), 1, nx + 1, RO, RO + ny, ny, 16)

    def whole(n, B, c):
        nx, ny, _ = n
        span = (1, nx + 1, RO, RO + ny)
        first_pass(B, work, (c,), (0,), *span, 16)
        sweep(C, XA, work, (c,), *span, ny, 16, False)
        sweep(XA, XB, work, (c,), *span, ny, 16, False)
        sweep(XB, XA, work, (c,), *span, ny, 16, False)
        sweep(XA, XB, work, (c,), *span, ny, 16, True)
        return restrict(XB, work, (c,), n, 0)

    whole_prepare(n3, K3, 0)
    gather_x(gb)
    place(K4, coarsen(K3, work, n3, 1), n4, 1)
    whole_prepare(n4, K4, 1)
    gather_end(1, gb, B3)
    place(B4, whole(n3, B3, 0), n4, 1)
    FIN[...] = whole(n4, B4, 1)
    row = FIN[pl.ds(gx * 8 + gy, 1), :]
    out_ref[0, :, :] = pltpu.roll(row, lax.rem(128 - 4 * gz, 128), 1)[:, :4]


def finish(fine, coarse, fine_out, coarse_out, buf, small, isem, osem):
    loads = [pltpu.make_async_copy(coarse, small, isem.at[4])]
    stores = [pltpu.make_async_copy(small, coarse_out, osem.at[4])]
    for j in range(4):
        part = pl.ds(8 * j, 8)
        loads.append(pltpu.make_async_copy(fine.at[part], buf.at[part], isem.at[j]))
        stores.append(pltpu.make_async_copy(buf.at[part], fine_out.at[part], osem.at[j]))
    start(loads)
    for load, store in zip(loads, stores):
        load.wait()
        store.start()
    for store in stores:
        store.wait()


def local(right_side, coefficient):
    def vm(*shape):
        return pltpu.VMEM(shape, F32)

    dma = pltpu.SemaphoreType.DMA
    scratch = [
        vm(44, 2, 64, 128), vm(44, 2, 64, 128),
        vm(28, 1, 48, 128), vm(28, 1, 48, 128),
        vm(20, 1, 40, 128), vm(20, 1, 40, 128),
        vm(34, 1, 64, 128), vm(34, 1, 64, 128),
        vm(18, 1, 48, 128), vm(18, 1, 48, 128),
        vm(6, 44, 2, 64, 128),
    ] + [vm(44, 2, 64, 128) for _ in range(5)] + [
        vm(16, 2, 64, 128), vm(2, 256, 128),
        vm(2, 2, 2, 32, 128), vm(2, 2, 4, 48, 128),
        vm(2, 2, 1, 16, 128), vm(2, 2, 3, 32, 128),
        vm(2, 6, 3, GZ, 8, 128), vm(2, GX, GY, 8, 128), vm(64, 128),
        dma((3,)), dma((4, 26)), dma((4, 26)), dma((2, 35)), dma((2, 35)), dma((2, 14)), dma((2, 14)),
    ]
    hbm = pl.BlockSpec(memory_space=pl.ANY)
    fine, coarse = pl.pallas_call(
        kernel,
        out_shape=(
            jax.ShapeDtypeStruct(right_side.shape, F32),
            jax.ShapeDtypeStruct((1, 1, 4), F32),
        ),
        in_specs=[hbm, hbm],
        out_specs=(hbm, pl.BlockSpec(memory_space=pltpu.VMEM)),
        scratch_shapes=scratch,
        compiler_params=pltpu.CompilerParams(
            collective_id=0, has_side_effects=True, vmem_limit_bytes=56 * 2**20),
        name="down_leg",
    )(right_side, coefficient)

    return pl.pallas_call(
        finish,
        out_shape=(
            jax.ShapeDtypeStruct(right_side.shape, F32),
            jax.ShapeDtypeStruct((1, 1, 4), F32),
        ),
        in_specs=[hbm, hbm],
        out_specs=(hbm, hbm),
        scratch_shapes=[vm(32, 32, 128), vm(1, 1, 4), dma((5,)), dma((5,))],
        compiler_params=pltpu.CompilerParams(vmem_limit_bytes=60 * 2**20),
        name="finish",
    )(fine, coarse)


def solution(mesh):
    placed = (P("gx", "gy", "gz"), P("gx", "gy", "gz"))
    return jax.shard_map(
        local, mesh=mesh, in_specs=placed, out_specs=placed, check_vma=False)
```
